768 devices in a mesh: ctx: 12 (over z_lo, core), ch: 64 (over z_hi, y, x).
Axes of the slice: x: 4, y: 8, z: 12 (z_hi: 2, z_lo: 6; z = z_hi * 6 + z_lo), core: 2. Of those that a mesh axis runs over, the one named last changes fastest.
Arguments:
- streams: bfloat16 [3, 4608, 3072], P(None, 'ch', 'ctx'), may hold values from -6 to 6
- short_taps: float32 [3, 4608, 3], P(None, 'ch'), may hold values from -1 to 1
- filter_in: float32 [32, 64], replicated, may hold values from -1 to 1
- filter_mid: float32 [64, 64], replicated, may hold values from -0.75 to 0.75
- filter_out: float32 [64, 4608], P(None, 'ch'), may hold values from -2 to 2
- decay_rate: float32 [4608], P('ch'), as said below
- skip_gain: float32 [4608], P('ch'), may hold values from 0.5 to 1.5
- out_weight: bfloat16 [4608, 4608], P('ch'), may hold values from -0.09375 to 0.09375
- grad_out: bfloat16 [4608, 3072], P('ch', 'ctx'), may hold values from -6 to 6
Outputs:
- layer_out: bfloat16 [4608, 3072], P('ch', 'ctx')
- grad_streams: bfloat16 [3, 4608, 3072], P(None, 'ch', 'ctx')
- grad_filter_in: float32 [32, 64], replicated
- grad_filter_mid: float32 [64, 64], replicated
- grad_filter_out: float32 [64, 4608], P(None, 'ch')
- grad_out_weight: float32 [4608, 4608], P('ch')
The draws below stay inside these ranges and needn't reach their ends.
Inputs may be any that keep to these rules, and one draw needn't show every extreme that they name: `decay_rate`: every channel's rate lies between 1 / 15360 and 1 / 30.
All inputs are finite; a program needn't handle non-finite values.
Results may differ from the reference program's by a relative error of at most 0.014.
Values may be sent and summed in bfloat16 or wider, within the bound.
No kernel may reach another device: no remote copies, remote signals or barrier semaphores. Data moves between devices by JAX's collectives and lax.ppermute only.
A program may use at most 64 MiB of HBM per device.

```python
import math
import jax
import jax.numpy as jnp
from jax import lax

CH = 4608
FH = 64
BANDS = 16
SHORT = 3
SEQ = 3072


def draw_decay_rate(key, part):
    pick_key, level_key = jax.random.split(jax.random.fold_in(key, 17))
    share = 0.5
    slower = jax.random.uniform(pick_key, (CH,)) < share
    lowest = jnp.where(slower, math.log(0.2), math.log(2.0))
    highest = jnp.where(slower, math.log(2.0), math.log(SEQ / 30.0))
    unit = jax.random.uniform(level_key, (CH,))
    return (jnp.exp(lowest + unit * (highest - lowest)) / SEQ).astype(jnp.float32)


def levels(rng, shape, cuts, least, top_value):
    level = 1.0
    for dim, shards_of in cuts:
        steps = jax.random.uniform(jax.random.fold_in(jax.random.fold_in(rng, 6), dim), (shards_of,), jnp.float32, least / len(cuts), top_value / len(cuts))
        level = level * jnp.repeat(jnp.exp(steps), shape[dim] // shards_of).reshape((-1,) + (1,) * (len(shape) - 1 - dim))
    return level


def gaussian(key, dims, spread, bound, cuts=(), kind=jnp.bfloat16):
    factor_of = levels(key, dims, cuts, -0.22, 0.18) if cuts else 1.0
    entries = jax.random.normal(key, dims, jnp.float32) * spread * factor_of
    return jnp.minimum(jnp.maximum(entries, -bound), bound).astype(kind)


def setup_inputs(seed: int = 0) -> dict:
    splits = jax.random.split(jax.random.key(seed), 10)
    return {
        "streams": gaussian(splits[0], (3, CH, SEQ), 1.0, 6.0, ((1, 64), (2, 12))),
        "short_taps": jnp.clip(jax.random.uniform(splits[1], (3, CH, SHORT), jnp.float32, -1.0, 1.0) * levels(splits[1], (3, CH, SHORT), ((1, 64),), -0.4, 0.0), -1.0, 1.0),
        "filter_in": gaussian(splits[2], (2 * BANDS, FH), (2 * BANDS) ** -0.5, 1.0, (), jnp.float32),
        "filter_mid": gaussian(splits[3], (FH, FH), FH ** -0.5, 0.75, (), jnp.float32),
        "filter_out": gaussian(splits[4], (FH, CH), (FH // 8) ** -0.5, 2.0, ((1, 64),), jnp.float32),
        "decay_rate": draw_decay_rate(jax.random.fold_in(splits[9], 71), 0),
        "skip_gain": jnp.clip(0.5 + 1.0 * jax.random.uniform(splits[6], (CH,), jnp.float32) ** levels(splits[6], (CH,), ((0, 64),), -0.2, 0.2), 0.5, 1.5),
        "out_weight": gaussian(splits[7], (CH, CH), CH ** -0.5, 0.09375, ((0, 64),)),
        "grad_out": gaussian(splits[8], (CH, SEQ), 1.0, 6.0, ((0, 64), (1, 12))),
    }


precise = lax.Precision.HIGHEST

def filter_values(filter_in, filter_mid, filter_out, decay_rate, length):
    band_count = filter_in.shape[0] // 2
    lag_index = jnp.arange(length).astype(jnp.int32)
    level_index = jnp.arange(1, band_count + 1).astype(jnp.int32)
    wrapped = level_index[:, None] * lag_index[None, :] % length
    phases = 2.0 * math.pi / length * wrapped.astype(jnp.float32)
    features = jnp.concatenate([jnp.cos(phases), jnp.sin(phases)], axis=0)
    hidden_one = jnp.sin(jnp.einsum('fh,fs->hs', filter_in, features, precision=precise))
    hidden_two = jnp.sin(jnp.einsum('gh,gs->hs', filter_mid, hidden_one, precision=precise))
    raw_out = jnp.einsum('hc,hs->cs', filter_out, hidden_two, precision=precise)
    lag_axis = lag_index.astype(jnp.float32)
    return raw_out * jnp.exp(-decay_rate[:, None] * lag_axis[None, :]) * jnp.sqrt(decay_rate)[:, None]

def short_apply(signal, short_taps):
    taps_width = short_taps.shape[2]
    length = signal.shape[2]
    padded = jnp.pad(signal.astype(jnp.float32), ((0, 0), (0, 0), (taps_width - 1, 0)))
    result = jnp.zeros(signal.shape, jnp.float32)
    for lag_step in range(taps_width):
        begin = taps_width - 1 - lag_step
        result = result + short_taps[:, :, lag_step:lag_step + 1] * padded[:, :, begin:begin + length]
    return result

def short_adjoint(signal, short_taps):
    taps_width = short_taps.shape[2]
    length = signal.shape[2]
    padded = jnp.pad(signal, ((0, 0), (0, 0), (0, taps_width - 1)))
    result = jnp.zeros(signal.shape, signal.dtype)
    for lag_step in range(taps_width):
        result = result + short_taps[:, :, lag_step:lag_step + 1] * padded[:, :, lag_step:lag_step + length]
    return result

def causal_apply(long_filter, signal):
    length = signal.shape[-1]
    spectrum = jnp.fft.rfft(long_filter, 2 * length) * jnp.fft.rfft(signal, 2 * length)
    return jnp.fft.irfft(spectrum, 2 * length)[..., :length]

def correlate(grad_signal, signal):
    length = signal.shape[-1]
    spectrum = jnp.fft.rfft(grad_signal, 2 * length) * jnp.conj(jnp.fft.rfft(signal, 2 * length))
    return jnp.fft.irfft(spectrum, 2 * length)[..., :length]

def reference(streams, short_taps, filter_in, filter_mid, filter_out, decay_rate, skip_gain, out_weight, grad_out):

    def make_filter(first_w, middle_w, last_w):
        return filter_values(first_w, middle_w, last_w, decay_rate, SEQ)
    long_filter, pullback = jax.vjp(make_filter, filter_in, filter_mid, filter_out)
    filtered = short_apply(streams, short_taps)
    product = (filtered[1] * filtered[2]).astype(jnp.bfloat16)
    product_wide = product.astype(jnp.float32)
    long_out = causal_apply(long_filter, product_wide) + skip_gain[:, None] * product_wide
    gated_out = (filtered[0] * long_out).astype(jnp.bfloat16)
    layer_out = jnp.dot(out_weight, gated_out, preferred_element_type=jnp.float32).astype(jnp.bfloat16)
    grad_out_weight = jnp.dot(grad_out, gated_out.T, preferred_element_type=jnp.float32)
    grad_gated = jnp.dot(out_weight.T, grad_out, preferred_element_type=jnp.float32).astype(jnp.bfloat16)
    grad_gated_wide = grad_gated.astype(jnp.float32)
    grad_long = (grad_gated_wide * filtered[0]).astype(jnp.bfloat16)
    grad_long_wide = grad_long.astype(jnp.float32)
    grad_first = grad_gated_wide * long_out
    flipped = causal_apply(long_filter, jnp.flip(grad_long_wide, -1))
    grad_product = jnp.flip(flipped, -1) + skip_gain[:, None] * grad_long_wide
    grad_lag = correlate(grad_long_wide, product_wide)
    grad_filtered = jnp.stack([grad_first, grad_product * filtered[2], grad_product * filtered[1]])
    grad_streams = short_adjoint(grad_filtered, short_taps).astype(jnp.bfloat16)
    grad_filter_in, grad_filter_mid, grad_filter_out = pullback(grad_lag)
    return (layer_out, grad_streams, grad_filter_in, grad_filter_mid, grad_filter_out, grad_out_weight)
```

```python
import functools
import math

import jax
import jax.numpy as jnp
import numpy as np
from jax import lax
from jax.experimental import pallas as pl
from jax.experimental.pallas import tpu as pltpu
from jax.sharding import PartitionSpec as P

f32 = jnp.float32
bf16 = jnp.bfloat16

BLOCK = 256
ROWS = 8
VMEM_LIMIT = 40 * 1024 * 1024


def split_table(table):
    high = table.astype(np.float32).astype(jnp.bfloat16)
    low = (table - high.astype(np.float64)).astype(np.float32).astype(jnp.bfloat16)
    return high, low


@functools.lru_cache(maxsize=None)
def transform_tables():
    frequency = np.arange(BLOCK)
    token = np.arange(BLOCK)
    angle = np.pi * ((2 * frequency[None, :] + 1) * token[:, None] % (4 * BLOCK)) / (2 * BLOCK)
    forward = np.concatenate([np.cos(angle), -np.sin(angle)], axis=1)
    return split_table(forward) + split_table(forward.T / BLOCK)


@functools.lru_cache(maxsize=None)
def position_features(band_count, length):
    wrapped = (np.arange(1, band_count + 1)[:, None] * np.arange(length)[None, :]) % length
    phases = 2.0 * np.pi / length * wrapped
    return np.concatenate([np.cos(phases), np.sin(phases)], axis=0).astype(np.float32)


def halves(value):
    high = value.astype(bf16)
    return high, (value - high.astype(f32)).astype(bf16)


def plain_dot(left, right, dims):
    return lax.dot_general(left, right, (dims, ((), ())), preferred_element_type=f32)


def close_dot(left, right, dims=((1,), (0,))):
    left_high, left_low = halves(left)
    right_high, right_low = halves(right)
    return (
        plain_dot(left_high, right_high, dims)
        + plain_dot(left_high, right_low, dims)
        + plain_dot(left_low, right_high, dims)
    )


def table_dot(left, high, low):
    dims = ((1,), (0,))
    if left.dtype == bf16:
        return plain_dot(left, high, dims) + plain_dot(left, low, dims)
    left_high, left_low = halves(left)
    return (
        plain_dot(left_high, high, dims)
        + plain_dot(left_high, low, dims)
        + plain_dot(left_low, high, dims)
    )


def sine_and_cosine(value):
    turns = jnp.floor(value * (2.0 / math.pi) + 0.5)
    rest = value - turns * 1.5703125
    rest = rest - turns * 4.837512969970703125e-4
    rest = rest - turns * 7.54978994876864e-8
    square = rest * rest
    sine = rest + rest * square * (
        -1.6666654611e-1 + square * (8.3321608736e-3 + square * -1.9515295891e-4)
    )
    cosine = (
        1.0
        - 0.5 * square
        + square
        * square
        * (4.166664568298827e-2 + square * (-1.388731625493765e-3 + square * 2.443315711809948e-5))
    )
    quadrant = turns.astype(jnp.int32)
    odd = (quadrant & 1) == 1
    sine_out = jnp.where(odd, cosine, sine)
    cosine_out = jnp.where(odd, sine, cosine)
    sine_out = jnp.where((quadrant & 2) == 2, -sine_out, sine_out)
    cosine_out = jnp.where(((quadrant + 1) & 2) == 2, -cosine_out, cosine_out)
    return sine_out, cosine_out


def envelope(decay, block):
    lag = (lax.broadcasted_iota(jnp.int32, (ROWS, BLOCK), 1) + block * BLOCK).astype(f32)
    return jnp.exp(-decay * lag) * jnp.sqrt(decay)


def parity():
    odd = lax.broadcasted_iota(jnp.int32, (ROWS, BLOCK), 1) & 1
    return (1 - 2 * odd).astype(f32)


DECAY, SKIP, OUT = 9, 10, 11


def network_kernel(
    features, filter_in, filter_mid, params, table_high, table_low,
    hidden_one, slope_one, hidden_two, slope_two, spectra, taps_scratch,
):
    count = features.shape[1] // BLOCK
    hidden = filter_in.shape[1]
    decay = params[:, DECAY : DECAY + 1]
    last = params[:, OUT : OUT + hidden]
    for block in range(count):
        at = slice(block * BLOCK, (block + 1) * BLOCK)
        sine, cosine = sine_and_cosine(
            close_dot(filter_in[...], features[:, at], ((0,), (0,)))
        )
        hidden_one[:, at] = sine
        slope_one[:, at] = cosine
        sine, cosine = sine_and_cosine(close_dot(filter_mid[...], sine, ((0,), (0,))))
        hidden_two[:, at] = sine
        slope_two[:, at] = cosine
        raw = close_dot(last, sine)
        taps_scratch[block * ROWS : (block + 1) * ROWS, :] = raw * envelope(decay, block)
    spectrum = table_dot(taps_scratch[...], table_high[...], table_low[...])
    sign = parity()
    for block in range(count):
        real = spectrum[block * ROWS : (block + 1) * ROWS, :BLOCK]
        imag = spectrum[block * ROWS : (block + 1) * ROWS, BLOCK:]
        if block:
            before = slice((block - 1) * ROWS, block * ROWS)
            real = real - sign * spectrum[before, BLOCK:]
            imag = imag + sign * spectrum[before, :BLOCK]
        spectra[block, :, :BLOCK] = real
        spectra[block, :, BLOCK:] = imag


def rows_of(value, rows):
    return value.reshape(value.shape[0] // rows, rows, value.shape[1])


def forward_kernel(
    blocks, params, spectra, table_high, table_low, back_high, back_low,
    gated, filtered, long_out, own_spectra, sums,
):
    count = blocks.shape[0]
    wide = 3 * ROWS
    raw = blocks[...].astype(f32).reshape(count * wide, BLOCK)
    lane = lax.broadcasted_iota(jnp.int32, (count * wide, BLOCK), 1)
    lead = jnp.zeros((wide, BLOCK), f32)
    shifted = [raw]
    for by in (1, 2):
        rolled = pltpu.roll(raw, by, 1)
        before = jnp.concatenate([lead, rolled[:-wide]], axis=0)
        shifted.append(jnp.where(lane < by, before, rolled))
    shifted = [rows_of(value, wide) for value in shifted]
    streams = []
    for stream in range(3):
        at = slice(stream * ROWS, (stream + 1) * ROWS)
        total = None
        for tap in range(3):
            column = stream * 3 + tap
            term = params[:, column : column + 1][None] * shifted[tap][:, at, :]
            total = term if total is None else total + term
        filtered[:, at, :] = total
        streams.append(total)
    product = (streams[1] * streams[2]).astype(bf16).astype(f32).reshape(count * ROWS, BLOCK)
    spectrum = table_dot(product.astype(bf16), table_high[...], table_low[...])
    own_spectra[...] = rows_of(spectrum, ROWS)
    for block in range(count):
        real = jnp.zeros((ROWS, BLOCK), f32)
        imag = jnp.zeros((ROWS, BLOCK), f32)
        for source in range(block + 1):
            filter_real = spectra[block - source, :, :BLOCK]
            filter_imag = spectra[block - source, :, BLOCK:]
            own_real = own_spectra[source, :, :BLOCK]
            own_imag = own_spectra[source, :, BLOCK:]
            real = real + filter_real * own_real - filter_imag * own_imag
            imag = imag + filter_real * own_imag + filter_imag * own_real
        sums[block * ROWS : (block + 1) * ROWS, :BLOCK] = real
        sums[block * ROWS : (block + 1) * ROWS, BLOCK:] = imag
    conv = table_dot(sums[...], back_high[...], back_low[...])
    skip = params[:, SKIP : SKIP + 1][None]
    result = rows_of(conv, ROWS) + skip * rows_of(product, ROWS)
    long_out[...] = result
    gated[...] = (streams[0] * result).reshape(count * ROWS, BLOCK).astype(bf16)


def backward_kernel(
    blocks, params, spectra, filtered, long_out, own_spectra,
    hidden_one, slope_one, hidden_two, slope_two, features, filter_mid,
    table_high, table_low, back_high, back_low,
    grad_streams, grad_shared, grad_last, sums, lag_sums, grad_spectra,
):
    count = blocks.shape[0]
    hidden = filter_mid.shape[0]
    wide = 3 * ROWS
    grad_gated = blocks[...].astype(f32)[:, ROWS : 2 * ROWS, :]
    query = filtered[:, :ROWS, :]
    grad_long = (grad_gated * query).reshape(count * ROWS, BLOCK).astype(bf16)
    spectrum = table_dot(grad_long, table_high[...], table_low[...])
    grad_spectra[...] = rows_of(spectrum, ROWS)
    sign = parity()
    after = None
    for block in reversed(range(count)):
        back_real = jnp.zeros((ROWS, BLOCK), f32)
        back_imag = jnp.zeros((ROWS, BLOCK), f32)
        lag_real = jnp.zeros((ROWS, BLOCK), f32)
        lag_imag = jnp.zeros((ROWS, BLOCK), f32)
        for target in range(block, count):
            grad_real = grad_spectra[target, :, :BLOCK]
            grad_imag = grad_spectra[target, :, BLOCK:]
            filter_real = spectra[target - block, :, :BLOCK]
            filter_imag = spectra[target - block, :, BLOCK:]
            back_real = back_real + filter_real * grad_real + filter_imag * grad_imag
            back_imag = back_imag + filter_real * grad_imag - filter_imag * grad_real
            own_real = own_spectra[target - block, :, :BLOCK]
            own_imag = own_spectra[target - block, :, BLOCK:]
            lag_real = lag_real + own_real * grad_real + own_imag * grad_imag
            lag_imag = lag_imag + own_real * grad_imag - own_imag * grad_real
        at = slice(block * ROWS, (block + 1) * ROWS)
        sums[at, :BLOCK] = back_real
        sums[at, BLOCK:] = back_imag
        if after is None:
            lag_sums[at, :BLOCK] = lag_real
            lag_sums[at, BLOCK:] = lag_imag
        else:
            lag_sums[at, :BLOCK] = lag_real + sign * after[1]
            lag_sums[at, BLOCK:] = lag_imag - sign * after[0]
        after = (lag_real, lag_imag)
    back = table_dot(sums[...], back_high[...], back_low[...])
    skip = params[:, SKIP : SKIP + 1][None]
    grad_product = rows_of(back, ROWS) + skip * rows_of(grad_long.astype(f32), ROWS)
    grads = [
        grad_gated * long_out[...],
        grad_product * filtered[:, 2 * ROWS :, :],
        grad_product * filtered[:, ROWS : 2 * ROWS, :],
    ]
    lane = lax.broadcasted_iota(jnp.int32, (count * ROWS, BLOCK), 1)
    tail = jnp.zeros((ROWS, BLOCK), f32)
    adjoint = []
    for stream in range(3):
        value = grads[stream].reshape(count * ROWS, BLOCK)
        total = params[:, stream * 3 : stream * 3 + 1][None] * grads[stream]
        for by in (1, 2):
            rolled = pltpu.roll(value, BLOCK - by, 1)
            following = jnp.concatenate([rolled[ROWS:], tail], axis=0)
            moved = jnp.where(lane >= BLOCK - by, following, rolled)
            column = stream * 3 + by
            total = total + params[:, column : column + 1][None] * rows_of(moved, ROWS)
        adjoint.append(total)
    half = BLOCK // 2
    packed = [part[:, :, :half] for part in adjoint] + [part[:, :, half:] for part in adjoint]
    grad_streams[...] = jnp.concatenate(packed, axis=1).astype(bf16)

    lags = table_dot(lag_sums[...], back_high[...], back_low[...])
    decay = params[:, DECAY : DECAY + 1]
    last = params[:, OUT : OUT + hidden]
    raw = [
        lags[block * ROWS : (block + 1) * ROWS] * envelope(decay, block)
        for block in range(count)
    ]
    total_last = jnp.zeros((ROWS, hidden), f32)
    total_mid = jnp.zeros((hidden, hidden), f32)
    total_in = jnp.zeros((features.shape[0], hidden), f32)
    across = ((1,), (1,))
    for block in range(count):
        at = slice(block * BLOCK, (block + 1) * BLOCK)
        total_last = total_last + close_dot(raw[block], hidden_two[:, at], across)
        grad_two = close_dot(last, raw[block], ((0,), (0,))) * slope_two[:, at]
        total_mid = total_mid + close_dot(hidden_one[:, at], grad_two, across)
        grad_one = close_dot(filter_mid[...], grad_two) * slope_one[:, at]
        total_in = total_in + close_dot(features[:, at], grad_one, across)
    high, low = halves(jnp.concatenate([total_in, total_mid], axis=0))
    grad_shared[...] = jnp.concatenate([high, low], axis=0)
    high, low = halves(total_last)
    grad_last[...] = jnp.concatenate([high.astype(f32), low.astype(f32)], axis=0).astype(bf16)


def call(kernel, outs, scratch, *operands):
    return pl.pallas_call(
        kernel,
        out_shape=[jax.ShapeDtypeStruct(shape, kind) for shape, kind in outs],
        in_specs=[pl.BlockSpec(memory_space=pltpu.VMEM)] * len(operands),
        out_specs=[pl.BlockSpec(memory_space=pltpu.VMEM)] * len(outs),
        scratch_shapes=[pltpu.VMEM(shape, kind) for shape, kind in scratch],
        compiler_params=pltpu.CompilerParams(vmem_limit_bytes=VMEM_LIMIT),
    )(*operands)


def exchange(value, axis, groups=None):
    return lax.all_to_all(value, axis, 0, 0, tiled=True, axis_index_groups=groups)


def shards(
    streams, short_taps, filter_in, filter_mid, filter_out, decay_rate, skip_gain, out_weight,
    grad_out,
):
    channels, tokens = streams.shape[1:]
    blocks = lax.axis_size("ctx")
    owners = lax.axis_size("ch")
    me = lax.axis_index("ctx")
    length = blocks * tokens
    share = channels // blocks
    hidden = filter_in.shape[1]
    band_rows = filter_in.shape[0]
    side = int(math.isqrt(owners))
    near = [[a * side + i for i in range(side)] for a in range(side)]
    far = [[a * side + i for a in range(side)] for i in range(side)]
    group = side * channels
    pad_rows = ROWS - share
    tables = [jnp.asarray(t) for t in transform_tables()]
    features = jnp.asarray(position_features(band_rows // 2, length))

    weight_parts = out_weight.reshape(channels, side, group).transpose(1, 0, 2)
    sent = jnp.concatenate(
        [jnp.broadcast_to(grad_out[None], (side, channels, tokens)), weight_parts], axis=2
    )
    sent = exchange(sent, "ch", far)
    cotangent = sent[:, :, :tokens].reshape(group, tokens)
    weight = sent[:, :, tokens:].reshape(group, group)
    grad_terms = lax.dot_general(
        weight, cotangent, (((0,), (0,)), ((), ())), preferred_element_type=f32
    ).astype(bf16)
    grad_terms = exchange(grad_terms.reshape(side, channels, tokens), "ch", near)
    grad_gated = jnp.sum(grad_terms.astype(f32), axis=0).astype(bf16)

    by_share = streams.reshape(3, blocks, share, tokens).transpose(1, 0, 2, 3)
    by_share = jnp.pad(by_share, ((0, 0), (0, 0), (0, pad_rows), (0, 0)))
    sequence = exchange(by_share.reshape(blocks, 3 * ROWS, tokens), "ctx")

    params = jnp.concatenate(
        [
            short_taps.transpose(1, 0, 2).reshape(channels, 9),
            decay_rate[:, None],
            skip_gain[:, None],
            filter_out.T,
        ],
        axis=1,
    )
    params = lax.dynamic_slice_in_dim(params, me * share, share, 0)
    params = jnp.pad(params, ((0, pad_rows), (0, 128 - params.shape[1])))

    wave = (hidden, length)
    hidden_one, slope_one, hidden_two, slope_two, spectra = call(
        network_kernel,
        [(wave, f32)] * 4 + [((blocks, ROWS, 2 * tokens), f32)],
        [((blocks * ROWS, tokens), f32)],
        features, filter_in, filter_mid, params, tables[0], tables[1],
    )
    gated, filtered, long_out, own_spectra = call(
        forward_kernel,
        [
            ((blocks * ROWS, tokens), bf16),
            ((blocks, 3 * ROWS, tokens), f32),
            ((blocks, ROWS, tokens), f32),
            ((blocks, ROWS, 2 * tokens), f32),
        ],
        [((blocks * ROWS, 2 * tokens), f32)],
        sequence, params, spectra, *tables,
    )

    turned = jnp.pad(grad_gated.reshape(blocks, share, tokens), ((0, 0), (0, pad_rows), (0, 0)))
    turned = jnp.concatenate([gated.reshape(blocks, ROWS, tokens), turned], axis=1)
    turned = exchange(turned, "ctx")
    own_gated = turned[:, :share, :].reshape(channels, tokens)

    grad_packed, grad_shared, grad_last = call(
        backward_kernel,
        [
            ((blocks, 6 * ROWS, tokens // 2), bf16),
            ((2 * (band_rows + hidden), hidden), bf16),
            ((2 * ROWS, hidden), bf16),
        ],
        [
            ((blocks * ROWS, 2 * tokens), f32),
            ((blocks * ROWS, 2 * tokens), f32),
            ((blocks, ROWS, 2 * tokens), f32),
        ],
        turned, params, spectra, filtered, long_out, own_spectra,
        hidden_one, slope_one, hidden_two, slope_two, features, filter_mid, *tables,
    )

    shared_rows = grad_shared.size // tokens
    sent = jnp.concatenate([own_gated, grad_shared.reshape(shared_rows, tokens)], axis=0)
    sent = exchange(
        jnp.broadcast_to(sent[None], (side,) + sent.shape), "ch", near
    )
    all_gated = sent[:, :channels].reshape(group, tokens)
    shared = jnp.sum(sent[:, channels:].astype(f32), axis=0)
    shared = shared[: shared_rows // 2] + shared[shared_rows // 2 :]

    out_terms = jnp.dot(weight, all_gated, preferred_element_type=f32).astype(bf16)
    by_block = cotangent.reshape(side, blocks, share, tokens).transpose(1, 0, 2, 3)
    weight_terms = lax.dot_general(
        by_block.reshape(group, tokens), all_gated, (((1,), (1,)), ((), ())),
        preferred_element_type=f32,
    ).astype(bf16)

    def both_halves(value):
        high = lax.reduce_precision(value, 8, 7)
        return high.astype(bf16), (value - high).astype(bf16)

    portion = (band_rows + hidden) // blocks
    high, low = both_halves(shared.reshape(blocks, portion, hidden))
    rows = side * share
    small = jnp.concatenate(
        [high, low, jnp.broadcast_to(grad_last[None], (blocks,) + grad_last.shape)], axis=1
    )
    small = jnp.pad(small, ((0, 0), (0, rows - small.shape[1]), (0, 0)))
    sent = jnp.concatenate([weight_terms.reshape(blocks, rows, group), small, grad_packed], axis=2)
    sent = exchange(sent, "ctx")
    weight_share = jnp.sum(sent[:, :, :group].astype(f32), axis=0).astype(bf16)
    small = sent[:, :, group : group + hidden].astype(f32)
    shared = jnp.sum(small[:, :portion] + small[:, portion : 2 * portion], axis=0)
    last_at = 2 * portion
    grad_last = small[:, last_at : last_at + share] + small[:, last_at + ROWS : last_at + ROWS + share]
    grad_filter_out = grad_last.reshape(channels, hidden).T
    packed = sent[:, :, group + hidden :].reshape(blocks, 2, 3, ROWS, tokens // 2)
    grad_streams = (
        packed[:, :, :, :share].transpose(2, 0, 3, 1, 4).reshape(3, channels, tokens)
    )

    high, low = both_halves(shared)
    width = 3 * tokens
    tail = jnp.concatenate([high, low], axis=0).reshape(2 * portion * hidden // tokens, tokens)
    weight_rows = jnp.pad(
        weight_share.reshape(side, share, group), ((0, 0), (0, 0), (0, width - group))
    ).reshape(side, share * 3, tokens)
    sent = jnp.concatenate(
        [
            out_terms.reshape(side, channels, tokens),
            weight_rows,
            jnp.broadcast_to(tail[None], (side,) + tail.shape),
        ],
        axis=1,
    )
    sent = exchange(sent, "ch", far)
    layer_out = jnp.sum(sent[:, :channels].astype(f32), axis=0).astype(bf16)
    weight_rows = sent[:, channels : channels + 3 * share].reshape(side, share, width)[:, :, :group]
    weight_rows = weight_rows.transpose(1, 0, 2).reshape(share, owners * channels)
    tail = jnp.sum(sent[:, channels + 3 * share :].astype(f32), axis=0)
    tail = tail.reshape(2, portion * hidden)
    high, low = both_halves(tail[0] + tail[1])

    tail = jnp.concatenate([high, low])
    spare = -tail.size % (share * 128)
    tail = jnp.pad(tail, (0, spare)).reshape(share, -1)
    sent = lax.all_gather(jnp.concatenate([weight_rows, tail], axis=1), "ctx", axis=0)
    grad_out_weight = sent[:, :, : weight_rows.shape[1]].reshape(channels, -1).astype(f32)
    tail = sent[:, :, weight_rows.shape[1] :].reshape(blocks, -1).astype(f32)
    size = portion * hidden
    shared = (tail[:, :size] + tail[:, size : 2 * size]).reshape(band_rows + hidden, hidden)
    return (
        layer_out, grad_streams, shared[:band_rows], shared[band_rows:], grad_filter_out,
        grad_out_weight,
    )


def solution(mesh):
    return jax.shard_map(
        shards,
        mesh=mesh,
        in_specs=(
            P(None, "ch", "ctx"),
            P(None, "ch", None),
            P(),
            P(),
            P(None, "ch"),
            P("ch"),
            P("ch"),
            P("ch", None),
            P("ch", "ctx"),
        ),
        out_specs=(P("ch", "ctx"), P(None, "ch", "ctx"), P(), P(), P(None, "ch"), P("ch", None)),
        check_vma=False,
    )
```

```python
import functools
import math

import jax
import jax.numpy as jnp
import numpy as np
from jax import lax
from jax.experimental import pallas as pl
from jax.experimental.pallas import tpu as pltpu
from jax.sharding import PartitionSpec as P

f32 = jnp.float32
bf16 = jnp.bfloat16

BLOCK = 256
ROWS = 8
VMEM_LIMIT = 16 * 1024 * 1024


def split_table(table):
    high = table.astype(np.float32).astype(jnp.bfloat16)
    low = (table - high.astype(np.float64)).astype(np.float32).astype(jnp.bfloat16)
    return high, low


@functools.lru_cache(maxsize=None)
def transform_tables():
    frequency = np.arange(BLOCK)
    token = np.arange(BLOCK)
    angle = np.pi * ((2 * frequency[None, :] + 1) * token[:, None] % (4 * BLOCK)) / (2 * BLOCK)
    forward = np.concatenate([np.cos(angle), -np.sin(angle)], axis=1)
    return split_table(forward) + split_table(forward.T / BLOCK)


@functools.lru_cache(maxsize=None)
def position_features(band_count, length):
    wrapped = (np.arange(1, band_count + 1)[:, None] * np.arange(length)[None, :]) % length
    phases = 2.0 * np.pi / length * wrapped
    return np.concatenate([np.cos(phases), np.sin(phases)], axis=0).astype(np.float32)


def halves(value):
    high = value.astype(bf16)
    return high, (value - high.astype(f32)).astype(bf16)


def plain_dot(left, right, dims):
    return lax.dot_general(left, right, (dims, ((), ())), preferred_element_type=f32)


def close_dot(left, right, dims=((1,), (0,))):
    left_high, left_low = halves(left)
    right_high, right_low = halves(right)
    return (
        plain_dot(left_high, right_high, dims)
        + plain_dot(left_high, right_low, dims)
        + plain_dot(left_low, right_high, dims)
    )


def table_dot(left, high, low):
    dims = ((1,), (0,))
    if left.dtype == bf16:
        return plain_dot(left, high, dims) + plain_dot(left, low, dims)
    left_high, left_low = halves(left)
    return (
        plain_dot(left_high, high, dims)
        + plain_dot(left_high, low, dims)
        + plain_dot(left_low, high, dims)
    )


def sine_and_cosine(value):
    turns = jnp.floor(value * (2.0 / math.pi) + 0.5)
    rest = value - turns * 1.5703125
    rest = rest - turns * 4.837512969970703125e-4
    rest = rest - turns * 7.54978994876864e-8
    square = rest * rest
    sine = rest + rest * square * (
        -1.6666654611e-1 + square * (8.3321608736e-3 + square * -1.9515295891e-4)
    )
    cosine = (
        1.0
        - 0.5 * square
        + square
        * square
        * (4.166664568298827e-2 + square * (-1.388731625493765e-3 + square * 2.443315711809948e-5))
    )
    quadrant = turns.astype(jnp.int32)
    odd = (quadrant & 1) == 1
    sine_out = jnp.where(odd, cosine, sine)
    cosine_out = jnp.where(odd, sine, cosine)
    sine_out = jnp.where((quadrant & 2) == 2, -sine_out, sine_out)
    cosine_out = jnp.where(((quadrant + 1) & 2) == 2, -cosine_out, cosine_out)
    return sine_out, cosine_out


def envelope(decay, block):
    lag = (lax.broadcasted_iota(jnp.int32, (ROWS, BLOCK), 1) + block * BLOCK).astype(f32)
    return jnp.exp(-decay * lag) * jnp.sqrt(decay)


def parity():
    odd = lax.broadcasted_iota(jnp.int32, (ROWS, BLOCK), 1) & 1
    return (1 - 2 * odd).astype(f32)


DECAY, SKIP, OUT = 9, 10, 11


def start_copies(pairs, semaphores):
    copies = [
        pltpu.make_async_copy(source, target, semaphores.at[i])
        for i, (source, target) in enumerate(pairs)
    ]
    for copy in copies:
        copy.start()
    return copies


def wait_copies(copies):
    for copy in copies:
        copy.wait()


def network_kernel(
    features, filter_in, filter_mid, params, table_high, table_low,
    kept_one, kept_slope_one, kept_two, kept_slope_two, kept_spectra,
    hidden_one, slope_one, hidden_two, slope_two, spectra, taps_scratch, semaphores,
):
    count = features.shape[1] // BLOCK
    hidden = filter_in.shape[1]
    decay = params[:, DECAY : DECAY + 1]
    last = params[:, OUT : OUT + hidden]
    for block in range(count):
        at = slice(block * BLOCK, (block + 1) * BLOCK)
        sine, cosine = sine_and_cosine(
            close_dot(filter_in[...], features[:, at], ((0,), (0,)))
        )
        hidden_one[:, at] = sine
        slope_one[:, at] = cosine
        sine, cosine = sine_and_cosine(close_dot(filter_mid[...], sine, ((0,), (0,))))
        hidden_two[:, at] = sine
        slope_two[:, at] = cosine
        raw = close_dot(last, sine)
        taps_scratch[block * ROWS : (block + 1) * ROWS, :] = raw * envelope(decay, block)
    copies = start_copies(
        [
            (hidden_one, kept_one),
            (slope_one, kept_slope_one),
            (hidden_two, kept_two),
            (slope_two, kept_slope_two),
        ],
        semaphores,
    )
    spectrum = table_dot(taps_scratch[...], table_high[...], table_low[...])
    sign = parity()
    for block in range(count):
        real = spectrum[block * ROWS : (block + 1) * ROWS, :BLOCK]
        imag = spectrum[block * ROWS : (block + 1) * ROWS, BLOCK:]
        if block:
            before = slice((block - 1) * ROWS, block * ROWS)
            real = real - sign * spectrum[before, BLOCK:]
            imag = imag + sign * spectrum[before, :BLOCK]
        spectra[block, :, :BLOCK] = real
        spectra[block, :, BLOCK:] = imag
    last_copy = pltpu.make_async_copy(spectra, kept_spectra, semaphores.at[4])
    last_copy.start()
    wait_copies(copies + [last_copy])


def rows_of(value, rows):
    return value.reshape(value.shape[0] // rows, rows, value.shape[1])


def forward_kernel(
    blocks, params, spectra, table_high, table_low, back_high, back_low,
    kept_gated, kept_filtered, kept_long_out, kept_spectra,
    gated, filtered, long_out, own_spectra, sums, semaphores,
):
    count = blocks.shape[0]
    wide = 3 * ROWS
    raw = blocks[...].astype(f32).reshape(count * wide, BLOCK)
    lane = lax.broadcasted_iota(jnp.int32, (count * wide, BLOCK), 1)
    lead = jnp.zeros((wide, BLOCK), f32)
    shifted = [raw]
    for by in (1, 2):
        rolled = pltpu.roll(raw, by, 1)
        before = jnp.concatenate([lead, rolled[:-wide]], axis=0)
        shifted.append(jnp.where(lane < by, before, rolled))
    shifted = [rows_of(value, wide) for value in shifted]
    streams = []
    for stream in range(3):
        at = slice(stream * ROWS, (stream + 1) * ROWS)
        total = None
        for tap in range(3):
            column = stream * 3 + tap
            term = params[:, column : column + 1][None] * shifted[tap][:, at, :]
            total = term if total is None else total + term
        filtered[:, at, :] = total
        streams.append(total)
    product = (streams[1] * streams[2]).astype(bf16).astype(f32).reshape(count * ROWS, BLOCK)
    spectrum = table_dot(product.astype(bf16), table_high[...], table_low[...])
    own_spectra[...] = rows_of(spectrum, ROWS)
    for block in range(count):
        real = jnp.zeros((ROWS, BLOCK), f32)
        imag = jnp.zeros((ROWS, BLOCK), f32)
        for source in range(block + 1):
            filter_real = spectra[block - source, :, :BLOCK]
            filter_imag = spectra[block - source, :, BLOCK:]
            own_real = own_spectra[source, :, :BLOCK]
            own_imag = own_spectra[source, :, BLOCK:]
            real = real + filter_real * own_real - filter_imag * own_imag
            imag = imag + filter_real * own_imag + filter_imag * own_real
        sums[block * ROWS : (block + 1) * ROWS, :BLOCK] = real
        sums[block * ROWS : (block + 1) * ROWS, BLOCK:] = imag
    conv = table_dot(sums[...], back_high[...], back_low[...])
    skip = params[:, SKIP : SKIP + 1][None]
    result = rows_of(conv, ROWS) + skip * rows_of(product, ROWS)
    long_out[...] = result
    gated[...] = (streams[0] * result).reshape(count * ROWS, BLOCK).astype(bf16)
    wait_copies(
        start_copies(
            [
                (gated, kept_gated),
                (filtered, kept_filtered),
                (long_out, kept_long_out),
                (own_spectra, kept_spectra),
            ],
            semaphores,
        )
    )


def backward_kernel(
    kept_spectra, kept_filtered, kept_long_out, kept_own_spectra,
    kept_one, kept_slope_one, kept_two, kept_slope_two,
    blocks, params, features, filter_mid, table_high, table_low, back_high, back_low,
    kept_grad_streams, grad_shared, grad_last,
    spectra, filtered, long_out, own_spectra, hidden_one, slope_one, hidden_two, slope_two,
    grad_streams, sums, lag_sums, grad_spectra, semaphores,
):
    copies = start_copies(
        [
            (kept_filtered, filtered),
            (kept_spectra, spectra),
            (kept_own_spectra, own_spectra),
            (kept_long_out, long_out),
            (kept_two, hidden_two),
            (kept_slope_two, slope_two),
            (kept_one, hidden_one),
            (kept_slope_one, slope_one),
        ],
        semaphores,
    )
    count = blocks.shape[0]
    hidden = filter_mid.shape[0]
    wide = 3 * ROWS
    grad_gated = blocks[...].astype(f32)[:, ROWS : 2 * ROWS, :]
    wait_copies(copies[:4])
    query = filtered[:, :ROWS, :]
    grad_long = (grad_gated * query).reshape(count * ROWS, BLOCK).astype(bf16)
    spectrum = table_dot(grad_long, table_high[...], table_low[...])
    grad_spectra[...] = rows_of(spectrum, ROWS)
    sign = parity()
    after = None
    for block in reversed(range(count)):
        back_real = jnp.zeros((ROWS, BLOCK), f32)
        back_imag = jnp.zeros((ROWS, BLOCK), f32)
        lag_real = jnp.zeros((ROWS, BLOCK), f32)
        lag_imag = jnp.zeros((ROWS, BLOCK), f32)
        for target in range(block, count):
            grad_real = grad_spectra[target, :, :BLOCK]
            grad_imag = grad_spectra[target, :, BLOCK:]
            filter_real = spectra[target - block, :, :BLOCK]
            filter_imag = spectra[target - block, :, BLOCK:]
            back_real = back_real + filter_real * grad_real + filter_imag * grad_imag
            back_imag = back_imag + filter_real * grad_imag - filter_imag * grad_real
            own_real = own_spectra[target - block, :, :BLOCK]
            own_imag = own_spectra[target - block, :, BLOCK:]
            lag_real = lag_real + own_real * grad_real + own_imag * grad_imag
            lag_imag = lag_imag + own_real * grad_imag - own_imag * grad_real
        at = slice(block * ROWS, (block + 1) * ROWS)
        sums[at, :BLOCK] = back_real
        sums[at, BLOCK:] = back_imag
        if after is None:
            lag_sums[at, :BLOCK] = lag_real
            lag_sums[at, BLOCK:] = lag_imag
        else:
            lag_sums[at, :BLOCK] = lag_real + sign * after[1]
            lag_sums[at, BLOCK:] = lag_imag - sign * after[0]
        after = (lag_real, lag_imag)
    back = table_dot(sums[...], back_high[...], back_low[...])
    skip = params[:, SKIP : SKIP + 1][None]
    grad_product = rows_of(back, ROWS) + skip * rows_of(grad_long.astype(f32), ROWS)
    grads = [
        grad_gated * long_out[...],
        grad_product * filtered[:, 2 * ROWS :, :],
        grad_product * filtered[:, ROWS : 2 * ROWS, :],
    ]
    lane = lax.broadcasted_iota(jnp.int32, (count * ROWS, BLOCK), 1)
    tail = jnp.zeros((ROWS, BLOCK), f32)
    adjoint = []
    for stream in range(3):
        value = grads[stream].reshape(count * ROWS, BLOCK)
        total = params[:, stream * 3 : stream * 3 + 1][None] * grads[stream]
        for by in (1, 2):
            rolled = pltpu.roll(value, BLOCK - by, 1)
            following = jnp.concatenate([rolled[ROWS:], tail], axis=0)
            moved = jnp.where(lane >= BLOCK - by, following, rolled)
            column = stream * 3 + by
            total = total + params[:, column : column + 1][None] * rows_of(moved, ROWS)
        adjoint.append(total)
    half = BLOCK // 2
    packed = [part[:, :, :half] for part in adjoint] + [part[:, :, half:] for part in adjoint]
    grad_streams[...] = jnp.concatenate(packed, axis=1).astype(bf16)
    streams_copy = pltpu.make_async_copy(grad_streams, kept_grad_streams, semaphores.at[8])
    streams_copy.start()
    wait_copies(copies[4:])

    lags = table_dot(lag_sums[...], back_high[...], back_low[...])
    decay = params[:, DECAY : DECAY + 1]
    last = params[:, OUT : OUT + hidden]
    raw = [
        lags[block * ROWS : (block + 1) * ROWS] * envelope(decay, block)
        for block in range(count)
    ]
    total_last = jnp.zeros((ROWS, hidden), f32)
    total_mid = jnp.zeros((hidden, hidden), f32)
    total_in = jnp.zeros((features.shape[0], hidden), f32)
    across = ((1,), (1,))
    for block in range(count):
        at = slice(block * BLOCK, (block + 1) * BLOCK)
        total_last = total_last + close_dot(raw[block], hidden_two[:, at], across)
        grad_two = close_dot(last, raw[block], ((0,), (0,))) * slope_two[:, at]
        total_mid = total_mid + close_dot(hidden_one[:, at], grad_two, across)
        grad_one = close_dot(filter_mid[...], grad_two) * slope_one[:, at]
        total_in = total_in + close_dot(features[:, at], grad_one, across)
    grad_shared[...] = jnp.concatenate([total_in, total_mid], axis=0).astype(bf16)
    high, low = halves(total_last)
    grad_last[...] = jnp.concatenate([high.astype(f32), low.astype(f32)], axis=0).astype(bf16)
    streams_copy.wait()


def pack_kernel(far_weight, far_cotangent, packed, weight, cotangent, semaphores):
    wait_copies(
        start_copies([(far_weight, weight), (far_cotangent, cotangent)], semaphores)
    )
    side = packed.shape[0]
    channels, tokens = cotangent.shape
    for i in range(side):
        packed[i, :, :tokens] = cotangent[...]
        pieces = [
            weight[:, (a * side + i) * channels : (a * side + i + 1) * channels]
            for a in range(side)
        ]
        packed[i, :, tokens:] = jnp.concatenate(pieces, axis=1)


NEAR, FAR = pltpu.VMEM, pltpu.HBM


def call(kernel, outs, scratch, copies, *operands):
    semaphores = [pltpu.SemaphoreType.DMA((copies,))] if copies else []
    return pl.pallas_call(
        kernel,
        out_shape=[
            pltpu.HBM(shape, kind) if place is FAR else jax.ShapeDtypeStruct(shape, kind)
            for place, shape, kind in outs
        ],
        in_specs=[pl.BlockSpec(memory_space=place) for place, _ in operands],
        out_specs=[pl.BlockSpec(memory_space=place) for place, _, _ in outs],
        scratch_shapes=[pltpu.VMEM(shape, kind) for shape, kind in scratch] + semaphores,
        compiler_params=pltpu.CompilerParams(vmem_limit_bytes=VMEM_LIMIT),
    )(
        *[
            pltpu.with_memory_space_constraint(operand, FAR) if place is FAR else operand
            for place, operand in operands
        ]
    )


def exchange(value, axis, groups=None):
    return lax.all_to_all(value, axis, 0, 0, tiled=True, axis_index_groups=groups)


def shards(
    streams, short_taps, filter_in, filter_mid, filter_out, decay_rate, skip_gain, out_weight,
    grad_out,
):
    channels, tokens = streams.shape[1:]
    blocks = lax.axis_size("ctx")
    owners = lax.axis_size("ch")
    me = lax.axis_index("ctx")
    length = blocks * tokens
    share = channels // blocks
    hidden = filter_in.shape[1]
    band_rows = filter_in.shape[0]
    side = int(math.isqrt(owners))
    near_groups = [[a * side + i for i in range(side)] for a in range(side)]
    far_groups = [[a * side + i for a in range(side)] for i in range(side)]
    group = side * channels
    pad_rows = ROWS - share
    tables = [jnp.asarray(t) for t in transform_tables()]
    features = jnp.asarray(position_features(band_rows // 2, length))

    (sent,) = call(
        pack_kernel,
        [(NEAR, (side, channels, tokens + group), bf16)],
        [(out_weight.shape, bf16), (grad_out.shape, bf16)],
        2,
        (FAR, out_weight), (FAR, grad_out),
    )
    sent = exchange(sent, "ch", near_groups)
    cotangent = sent[:, :, :tokens].reshape(group, tokens)
    weight = sent[:, :, tokens:].reshape(group, group)
    grad_terms = lax.dot_general(
        weight, cotangent, (((0,), (0,)), ((), ())), preferred_element_type=f32
    ).astype(bf16)
    grad_terms = exchange(grad_terms.reshape(side, channels, tokens), "ch", far_groups)
    grad_gated = jnp.sum(grad_terms.astype(f32), axis=0).astype(bf16)

    by_share = streams.reshape(3, blocks, share, tokens).transpose(1, 0, 2, 3)
    by_share = jnp.pad(by_share, ((0, 0), (0, 0), (0, pad_rows), (0, 0)))
    sequence = exchange(by_share.reshape(blocks, 3 * ROWS, tokens), "ctx")

    params = jnp.concatenate(
        [
            short_taps.transpose(1, 0, 2).reshape(channels, 9),
            decay_rate[:, None],
            skip_gain[:, None],
            filter_out.T,
        ],
        axis=1,
    )
    params = lax.dynamic_slice_in_dim(params, me * share, share, 0)
    params = jnp.pad(params, ((0, pad_rows), (0, 128 - params.shape[1])))

    def near(*values):
        return [(NEAR, value) for value in values]

    def far_like(shapes):
        return [(FAR,) + shape for shape in shapes]

    wave = ((hidden, length), f32)
    spectrum = ((blocks, ROWS, 2 * tokens), f32)
    kept_waves = [wave] * 4 + [spectrum]
    *waves, spectra = call(
        network_kernel, far_like(kept_waves), kept_waves + [((blocks * ROWS, tokens), f32)], 5,
        *near(features, filter_in, filter_mid, params, tables[0], tables[1]),
    )
    kept = [
        ((blocks * ROWS, tokens), bf16),
        ((blocks, 3 * ROWS, tokens), f32),
        ((blocks, ROWS, tokens), f32),
        spectrum,
    ]
    gated, filtered, long_out, own_spectra = call(
        forward_kernel, far_like(kept), kept + [((blocks * ROWS, 2 * tokens), f32)], 4,
        *near(sequence, params, spectra, *tables),
    )

    turned = jnp.pad(grad_gated.reshape(blocks, share, tokens), ((0, 0), (0, pad_rows), (0, 0)))
    turned = jnp.concatenate([gated.reshape(blocks, ROWS, tokens), turned], axis=1)
    turned = exchange(turned, "ctx")
    own_gated = turned[:, :share, :].reshape(channels, tokens)

    packed_streams = ((blocks, 6 * ROWS, tokens // 2), bf16)
    grad_packed, grad_shared, grad_last = call(
        backward_kernel,
        [
            (FAR,) + packed_streams,
            (NEAR, (band_rows + hidden, hidden), bf16),
            (NEAR, (2 * ROWS, hidden), bf16),
        ],
        [spectrum, kept[1], kept[2], spectrum]
        + [wave] * 4
        + [packed_streams]
        + [((blocks * ROWS, 2 * tokens), f32)] * 2
        + [spectrum],
        9,
        *[(FAR, value) for value in (spectra, filtered, long_out, own_spectra, *waves)],
        *near(turned, params, features, filter_mid, *tables),
    )

    shared_rows = grad_shared.size // tokens
    sent = jnp.concatenate([own_gated, grad_shared.reshape(shared_rows, tokens)], axis=0)
    sent = exchange(
        jnp.broadcast_to(sent[None], (side,) + sent.shape), "ch", far_groups
    )
    all_gated = sent[:, :channels].reshape(group, tokens)
    shared = jnp.sum(sent[:, channels:].astype(f32), axis=0)

    out_terms = jnp.dot(weight, all_gated, preferred_element_type=f32).astype(bf16)
    def both_halves(value):
        high = lax.reduce_precision(value, 8, 7)
        return high.astype(bf16), (value - high).astype(bf16)

    chips = blocks // 2
    core = me % 2
    rows = side * share
    portion = (band_rows + hidden) // blocks
    by_core = cotangent.reshape(side, chips, 2, share, tokens).transpose(2, 1, 0, 3, 4)
    shared = shared.reshape(chips, 2, portion, hidden)
    grad_packed = grad_packed.reshape((chips, 2) + grad_packed.shape[1:])

    def parts_for(which):
        left = lax.dynamic_index_in_dim(by_core, which, 0, False).reshape(chips * rows, tokens)
        terms = lax.dot_general(
            left, all_gated, (((1,), (1,)), ((), ())), preferred_element_type=f32
        ).reshape(chips, rows, group)
        return (
            terms,
            lax.dynamic_index_in_dim(shared, which, 1, False),
            lax.dynamic_index_in_dim(grad_packed, which, 1, False),
        )

    def joined(terms, shared, lasts, packed):
        high, low = both_halves(shared)
        small = jnp.concatenate([high, low] + lasts, axis=1)
        small = jnp.pad(small, ((0, 0), (0, rows - small.shape[1]), (0, 0)))
        return jnp.concatenate([terms.astype(bf16), small] + packed, axis=2)

    last_here = jnp.broadcast_to(grad_last[None], (chips,) + grad_last.shape)
    terms, shared_part, packed = parts_for(1 - core)
    sent = joined(terms, shared_part, [last_here], [packed])
    sent = lax.ppermute(sent, "ctx", [(k, k ^ 1) for k in range(blocks)])
    terms, shared_part, packed = parts_for(core)
    terms = terms + sent[:, :, :group].astype(f32)
    small = sent[:, :, group : group + hidden]
    shared_part = (
        shared_part
        + small[:, :portion].astype(f32)
        + small[:, portion : 2 * portion].astype(f32)
    )
    last_at = 2 * portion
    last_there = small[:, last_at : last_at + 2 * ROWS]
    packed_there = sent[:, :, group + hidden :]
    second = core == 1

    def in_order(here, there):
        return [jnp.where(second, there, here), jnp.where(second, here, there)]

    sent = joined(
        terms, shared_part, in_order(last_here, last_there), in_order(packed, packed_there)
    )
    sent = exchange(sent, "ctx", [[2 * z + c for z in range(chips)] for c in range(2)])
    weight_share = jnp.sum(sent[:, :, :group].astype(f32), axis=0).astype(bf16)
    small = sent[:, :, group : group + hidden].astype(f32)
    shared = jnp.sum(small[:, :portion] + small[:, portion : 2 * portion], axis=0)
    lasts = small[:, last_at : last_at + 4 * ROWS].reshape(blocks, 2, ROWS, hidden)[:, :, :share]
    grad_filter_out = jnp.sum(lasts, axis=1).reshape(channels, hidden).T
    packed = sent[:, :, group + hidden :].reshape(chips, 2, 3, ROWS, 2, tokens // 2)
    grad_streams = (
        packed[:, :, :, :share].transpose(2, 0, 4, 3, 1, 5).reshape(3, channels, tokens)
    )

    high, low = both_halves(shared)
    width = 3 * tokens
    tail = jnp.concatenate([high, low], axis=0).reshape(2 * portion * hidden // tokens, tokens)
    weight_rows = jnp.pad(
        weight_share.reshape(side, share, group), ((0, 0), (0, 0), (0, width - group))
    ).reshape(side, share * 3, tokens)
    sent = jnp.concatenate(
        [
            out_terms.reshape(side, channels, tokens),
            weight_rows,
            jnp.broadcast_to(tail[None], (side,) + tail.shape),
        ],
        axis=1,
    )
    sent = exchange(sent, "ch", near_groups)
    layer_out = jnp.sum(sent[:, :channels].astype(f32), axis=0).astype(bf16)
    weight_rows = sent[:, channels : channels + 3 * share].reshape(side, share, width)[:, :, :group]
    weight_rows = weight_rows.reshape(side, share, side, channels).transpose(1, 2, 0, 3)
    weight_rows = weight_rows.reshape(share, owners * channels)
    tail = jnp.sum(sent[:, channels + 3 * share :].astype(f32), axis=0)
    tail = tail.reshape(2, portion * hidden)
    high, low = both_halves(tail[0] + tail[1])

    tail = jnp.concatenate([high, low])
    spare = -tail.size % (share * 128)
    tail = jnp.pad(tail, (0, spare)).reshape(share, -1)
    sent = lax.all_gather(jnp.concatenate([weight_rows, tail], axis=1), "ctx", axis=0)
    grad_out_weight = sent[:, :, : weight_rows.shape[1]].reshape(channels, -1).astype(f32)
    tail = sent[:, :, weight_rows.shape[1] :].reshape(blocks, -1).astype(f32)
    size = portion * hidden
    shared = (tail[:, :size] + tail[:, size : 2 * size]).reshape(band_rows + hidden, hidden)
    return (
        layer_out, grad_streams, shared[:band_rows], shared[band_rows:], grad_filter_out,
        grad_out_weight,
    )


def solution(mesh):
    return jax.shard_map(
        shards,
        mesh=mesh,
        in_specs=(
            P(None, "ch", "ctx"),
            P(None, "ch", None),
            P(),
            P(),
            P(None, "ch"),
            P("ch"),
            P("ch"),
            P("ch", None),
            P("ch", "ctx"),
        ),
        out_specs=(P("ch", "ctx"), P(None, "ch", "ctx"), P(), P(), P(None, "ch"), P("ch", None)),
        check_vma=False,
    )
```

```python
import functools
import math

import jax
import jax.numpy as jnp
import numpy as np
from jax import lax
from jax.experimental import pallas as pl
from jax.experimental.pallas import tpu as pltpu
from jax.sharding import PartitionSpec as P

f32 = jnp.float32
bf16 = jnp.bfloat16

BLOCK = 256
ROWS = 8
VMEM_LIMIT = 16 * 1024 * 1024


def split_table(table):
    high = table.astype(np.float32).astype(jnp.bfloat16)
    low = (table - high.astype(np.float64)).astype(np.float32).astype(jnp.bfloat16)
    return high, low


@functools.lru_cache(maxsize=None)
def transform_tables():
    frequency = np.arange(BLOCK)
    token = np.arange(BLOCK)
    angle = np.pi * ((2 * frequency[None, :] + 1) * token[:, None] % (4 * BLOCK)) / (2 * BLOCK)
    forward = np.concatenate([np.cos(angle), -np.sin(angle)], axis=1)
    return split_table(forward) + split_table(forward.T / BLOCK)


@functools.lru_cache(maxsize=None)
def position_features(band_count, length):
    wrapped = (np.arange(1, band_count + 1)[:, None] * np.arange(length)[None, :]) % length
    phases = 2.0 * np.pi / length * wrapped
    return np.concatenate([np.cos(phases), np.sin(phases)], axis=0).astype(np.float32)


def halves(value):
    high = value.astype(bf16)
    return high, (value - high.astype(f32)).astype(bf16)


def plain_dot(left, right, dims):
    return lax.dot_general(left, right, (dims, ((), ())), preferred_element_type=f32)


def close_dot(left, right, dims=((1,), (0,))):
    left_high, left_low = halves(left)
    right_high, right_low = halves(right)
    return (
        plain_dot(left_high, right_high, dims)
        + plain_dot(left_high, right_low, dims)
        + plain_dot(left_low, right_high, dims)
    )


def table_dot(left, high, low):
    dims = ((1,), (0,))
    if left.dtype == bf16:
        return plain_dot(left, high, dims) + plain_dot(left, low, dims)
    left_high, left_low = halves(left)
    return (
        plain_dot(left_high, high, dims)
        + plain_dot(left_high, low, dims)
        + plain_dot(left_low, high, dims)
    )


def sine_and_cosine(value):
    turns = jnp.floor(value * (2.0 / math.pi) + 0.5)
    rest = value - turns * 1.5703125
    rest = rest - turns * 4.837512969970703125e-4
    rest = rest - turns * 7.54978994876864e-8
    square = rest * rest
    sine = rest + rest * square * (
        -1.6666654611e-1 + square * (8.3321608736e-3 + square * -1.9515295891e-4)
    )
    cosine = (
        1.0
        - 0.5 * square
        + square
        * square
        * (4.166664568298827e-2 + square * (-1.388731625493765e-3 + square * 2.443315711809948e-5))
    )
    quadrant = turns.astype(jnp.int32)
    odd = (quadrant & 1) == 1
    sine_out = jnp.where(odd, cosine, sine)
    cosine_out = jnp.where(odd, sine, cosine)
    sine_out = jnp.where((quadrant & 2) == 2, -sine_out, sine_out)
    cosine_out = jnp.where(((quadrant + 1) & 2) == 2, -cosine_out, cosine_out)
    return sine_out, cosine_out


def envelope(decay, block):
    lag = (lax.broadcasted_iota(jnp.int32, (ROWS, BLOCK), 1) + block * BLOCK).astype(f32)
    return jnp.exp(-decay * lag) * jnp.sqrt(decay)


def parity():
    odd = lax.broadcasted_iota(jnp.int32, (ROWS, BLOCK), 1) & 1
    return (1 - 2 * odd).astype(f32)


DECAY, SKIP, OUT = 9, 10, 11


def start_copies(pairs, semaphores):
    copies = [
        pltpu.make_async_copy(source, target, semaphores.at[i])
        for i, (source, target) in enumerate(pairs)
    ]
    for copy in copies:
        copy.start()
    return copies


def wait_copies(copies):
    for copy in copies:
        copy.wait()


def network_kernel(
    features, filter_in, filter_mid, params, table_high, table_low,
    kept_one, kept_slope_one, kept_two, kept_slope_two, kept_spectra,
    hidden_one, slope_one, hidden_two, slope_two, spectra, taps_scratch, semaphores,
):
    count = features.shape[1] // BLOCK
    hidden = filter_in.shape[1]
    decay = params[:, DECAY : DECAY + 1]
    last = params[:, OUT : OUT + hidden]
    for block in range(count):
        at = slice(block * BLOCK, (block + 1) * BLOCK)
        sine, cosine = sine_and_cosine(
            close_dot(filter_in[...], features[:, at], ((0,), (0,)))
        )
        hidden_one[:, at] = sine
        slope_one[:, at] = cosine
        sine, cosine = sine_and_cosine(close_dot(filter_mid[...], sine, ((0,), (0,))))
        hidden_two[:, at] = sine
        slope_two[:, at] = cosine
        raw = close_dot(last, sine)
        taps_scratch[block * ROWS : (block + 1) * ROWS, :] = raw * envelope(decay, block)
    copies = start_copies(
        [
            (hidden_one, kept_one),
            (slope_one, kept_slope_one),
            (hidden_two, kept_two),
            (slope_two, kept_slope_two),
        ],
        semaphores,
    )
    spectrum = table_dot(taps_scratch[...], table_high[...], table_low[...])
    sign = parity()
    for block in range(count):
        real = spectrum[block * ROWS : (block + 1) * ROWS, :BLOCK]
        imag = spectrum[block * ROWS : (block + 1) * ROWS, BLOCK:]
        if block:
            before = slice((block - 1) * ROWS, block * ROWS)
            real = real - sign * spectrum[before, BLOCK:]
            imag = imag + sign * spectrum[before, :BLOCK]
        spectra[block, :, :BLOCK] = real
        spectra[block, :, BLOCK:] = imag
    last_copy = pltpu.make_async_copy(spectra, kept_spectra, semaphores.at[4])
    last_copy.start()
    wait_copies(copies + [last_copy])


def rows_of(value, rows):
    return value.reshape(value.shape[0] // rows, rows, value.shape[1])


def forward_kernel(
    blocks, params, spectra, table_high, table_low, back_high, back_low,
    kept_gated, kept_filtered, kept_long_out, kept_spectra,
    gated, filtered, long_out, own_spectra, sums, semaphores,
):
    count = blocks.shape[0]
    wide = 3 * ROWS
    raw = blocks[...].astype(f32).reshape(count * wide, BLOCK)
    lane = lax.broadcasted_iota(jnp.int32, (count * wide, BLOCK), 1)
    lead = jnp.zeros((wide, BLOCK), f32)
    shifted = [raw]
    for by in (1, 2):
        rolled = pltpu.roll(raw, by, 1)
        before = jnp.concatenate([lead, rolled[:-wide]], axis=0)
        shifted.append(jnp.where(lane < by, before, rolled))
    shifted = [rows_of(value, wide) for value in shifted]
    streams = []
    for stream in range(3):
        at = slice(stream * ROWS, (stream + 1) * ROWS)
        total = None
        for tap in range(3):
            column = stream * 3 + tap
            term = params[:, column : column + 1][None] * shifted[tap][:, at, :]
            total = term if total is None else total + term
        filtered[:, at, :] = total
        streams.append(total)
    product = (streams[1] * streams[2]).astype(bf16).astype(f32).reshape(count * ROWS, BLOCK)
    spectrum = table_dot(product.astype(bf16), table_high[...], table_low[...])
    own_spectra[...] = rows_of(spectrum, ROWS)
    for block in range(count):
        real = jnp.zeros((ROWS, BLOCK), f32)
        imag = jnp.zeros((ROWS, BLOCK), f32)
        for source in range(block + 1):
            filter_real = spectra[block - source, :, :BLOCK]
            filter_imag = spectra[block - source, :, BLOCK:]
            own_real = own_spectra[source, :, :BLOCK]
            own_imag = own_spectra[source, :, BLOCK:]
            real = real + filter_real * own_real - filter_imag * own_imag
            imag = imag + filter_real * own_imag + filter_imag * own_real
        sums[block * ROWS : (block + 1) * ROWS, :BLOCK] = real
        sums[block * ROWS : (block + 1) * ROWS, BLOCK:] = imag
    conv = table_dot(sums[...], back_high[...], back_low[...])
    skip = params[:, SKIP : SKIP + 1][None]
    result = rows_of(conv, ROWS) + skip * rows_of(product, ROWS)
    long_out[...] = result
    gated[...] = (streams[0] * result).reshape(count * ROWS, BLOCK).astype(bf16)
    wait_copies(
        start_copies(
            [
                (gated, kept_gated),
                (filtered, kept_filtered),
                (long_out, kept_long_out),
                (own_spectra, kept_spectra),
            ],
            semaphores,
        )
    )


def backward_kernel(
    kept_spectra, kept_filtered, kept_long_out, kept_own_spectra,
    kept_one, kept_slope_one, kept_two, kept_slope_two,
    blocks, params, features, filter_mid, table_high, table_low, back_high, back_low,
    kept_grad_streams, grad_shared, grad_last,
    spectra, filtered, long_out, own_spectra, hidden_one, slope_one, hidden_two, slope_two,
    grad_streams, sums, lag_sums, grad_spectra, semaphores,
):
    copies = start_copies(
        [
            (kept_filtered, filtered),
            (kept_spectra, spectra),
            (kept_own_spectra, own_spectra),
            (kept_long_out, long_out),
            (kept_two, hidden_two),
            (kept_slope_two, slope_two),
            (kept_one, hidden_one),
            (kept_slope_one, slope_one),
        ],
        semaphores,
    )
    count = blocks.shape[0]
    hidden = filter_mid.shape[0]
    wide = 3 * ROWS
    grad_gated = blocks[...].astype(f32)[:, ROWS : 2 * ROWS, :]
    wait_copies(copies[:4])
    query = filtered[:, :ROWS, :]
    grad_long = (grad_gated * query).reshape(count * ROWS, BLOCK).astype(bf16)
    spectrum = table_dot(grad_long, table_high[...], table_low[...])
    grad_spectra[...] = rows_of(spectrum, ROWS)
    sign = parity()
    after = None
    for block in reversed(range(count)):
        back_real = jnp.zeros((ROWS, BLOCK), f32)
        back_imag = jnp.zeros((ROWS, BLOCK), f32)
        lag_real = jnp.zeros((ROWS, BLOCK), f32)
        lag_imag = jnp.zeros((ROWS, BLOCK), f32)
        for target in range(block, count):
            grad_real = grad_spectra[target, :, :BLOCK]
            grad_imag = grad_spectra[target, :, BLOCK:]
            filter_real = spectra[target - block, :, :BLOCK]
            filter_imag = spectra[target - block, :, BLOCK:]
            back_real = back_real + filter_real * grad_real + filter_imag * grad_imag
            back_imag = back_imag + filter_real * grad_imag - filter_imag * grad_real
            own_real = own_spectra[target - block, :, :BLOCK]
            own_imag = own_spectra[target - block, :, BLOCK:]
            lag_real = lag_real + own_real * grad_real + own_imag * grad_imag
            lag_imag = lag_imag + own_real * grad_imag - own_imag * grad_real
        at = slice(block * ROWS, (block + 1) * ROWS)
        sums[at, :BLOCK] = back_real
        sums[at, BLOCK:] = back_imag
        if after is None:
            lag_sums[at, :BLOCK] = lag_real
            lag_sums[at, BLOCK:] = lag_imag
        else:
            lag_sums[at, :BLOCK] = lag_real + sign * after[1]
            lag_sums[at, BLOCK:] = lag_imag - sign * after[0]
        after = (lag_real, lag_imag)
    back = table_dot(sums[...], back_high[...], back_low[...])
    skip = params[:, SKIP : SKIP + 1][None]
    grad_product = rows_of(back, ROWS) + skip * rows_of(grad_long.astype(f32), ROWS)
    grads = [
        grad_gated * long_out[...],
        grad_product * filtered[:, 2 * ROWS :, :],
        grad_product * filtered[:, ROWS : 2 * ROWS, :],
    ]
    lane = lax.broadcasted_iota(jnp.int32, (count * ROWS, BLOCK), 1)
    tail = jnp.zeros((ROWS, BLOCK), f32)
    adjoint = []
    for stream in range(3):
        value = grads[stream].reshape(count * ROWS, BLOCK)
        total = params[:, stream * 3 : stream * 3 + 1][None] * grads[stream]
        for by in (1, 2):
            rolled = pltpu.roll(value, BLOCK - by, 1)
            following = jnp.concatenate([rolled[ROWS:], tail], axis=0)
            moved = jnp.where(lane >= BLOCK - by, following, rolled)
            column = stream * 3 + by
            total = total + params[:, column : column + 1][None] * rows_of(moved, ROWS)
        adjoint.append(total)
    half = BLOCK // 2
    packed = [part[:, :, :half] for part in adjoint] + [part[:, :, half:] for part in adjoint]
    grad_streams[...] = jnp.concatenate(packed, axis=1).astype(bf16)
    streams_copy = pltpu.make_async_copy(grad_streams, kept_grad_streams, semaphores.at[8])
    streams_copy.start()
    wait_copies(copies[4:])

    lags = table_dot(lag_sums[...], back_high[...], back_low[...])
    decay = params[:, DECAY : DECAY + 1]
    last = params[:, OUT : OUT + hidden]
    raw = [
        lags[block * ROWS : (block + 1) * ROWS] * envelope(decay, block)
        for block in range(count)
    ]
    total_last = jnp.zeros((ROWS, hidden), f32)
    total_mid = jnp.zeros((hidden, hidden), f32)
    total_in = jnp.zeros((features.shape[0], hidden), f32)
    across = ((1,), (1,))
    for block in range(count):
        at = slice(block * BLOCK, (block + 1) * BLOCK)
        total_last = total_last + close_dot(raw[block], hidden_two[:, at], across)
        grad_two = close_dot(last, raw[block], ((0,), (0,))) * slope_two[:, at]
        total_mid = total_mid + close_dot(hidden_one[:, at], grad_two, across)
        grad_one = close_dot(filter_mid[...], grad_two) * slope_one[:, at]
        total_in = total_in + close_dot(features[:, at], grad_one, across)
    grad_shared[...] = jnp.concatenate([total_in, total_mid], axis=0).astype(bf16)
    high, low = halves(total_last)
    grad_last[...] = jnp.concatenate([high.astype(f32), low.astype(f32)], axis=0).astype(bf16)
    streams_copy.wait()


def pack_kernel(far_weight, far_cotangent, packed, weight, cotangent, semaphores):
    wait_copies(
        start_copies([(far_weight, weight), (far_cotangent, cotangent)], semaphores)
    )
    side = packed.shape[0]
    channels, tokens = cotangent.shape
    order = [half * (side // 2) + place for place in range(side // 2) for half in range(2)]
    for i in range(side):
        packed[i, :, :tokens] = cotangent[...]
        pieces = [
            weight[:, (a * side + i) * channels : (a * side + i + 1) * channels]
            for a in order
        ]
        packed[i, :, tokens:] = jnp.concatenate(pieces, axis=1)


NEAR, FAR = pltpu.VMEM, pltpu.HBM


def call(kernel, flops, outs, scratch, copies, *operands):
    semaphores = [pltpu.SemaphoreType.DMA((copies,))] if copies else []
    return pl.pallas_call(
        kernel,
        out_shape=[
            pltpu.HBM(shape, kind) if place is FAR else jax.ShapeDtypeStruct(shape, kind)
            for place, shape, kind in outs
        ],
        in_specs=[pl.BlockSpec(memory_space=place) for place, _ in operands],
        out_specs=[pl.BlockSpec(memory_space=place) for place, _, _ in outs],
        scratch_shapes=[pltpu.VMEM(shape, kind) for shape, kind in scratch] + semaphores,
        compiler_params=pltpu.CompilerParams(vmem_limit_bytes=VMEM_LIMIT),
        cost_estimate=pl.CostEstimate(
            flops=flops, bytes_accessed=4 * 1024 * 1024, transcendentals=0
        ),
    )(
        *[
            pltpu.with_memory_space_constraint(operand, FAR) if place is FAR else operand
            for place, operand in operands
        ]
    )


def exchange(value, axis, groups=None):
    return lax.all_to_all(value, axis, 0, 0, tiled=True, axis_index_groups=groups)


def shards(
    streams, short_taps, filter_in, filter_mid, filter_out, decay_rate, skip_gain, out_weight,
    grad_out,
):
    channels, tokens = streams.shape[1:]
    blocks = lax.axis_size("ctx")
    owners = lax.axis_size("ch")
    me = lax.axis_index("ctx")
    length = blocks * tokens
    share = channels // blocks
    hidden = filter_in.shape[1]
    band_rows = filter_in.shape[0]
    side = int(math.isqrt(owners))
    near_groups = [[a * side + i for i in range(side)] for a in range(side)]
    places = side // 2
    place_groups = [
        [(half * places + place) * side + i for place in range(places)]
        for half in range(2)
        for i in range(side)
    ]
    half = lax.axis_index("ch") // (places * side)

    def other_half(value):
        pairs = [(j, (j + places * side) % owners) for j in range(owners)]
        return lax.ppermute(value, "ch", pairs)

    group = side * channels
    pad_rows = ROWS - share
    tables = [jnp.asarray(t) for t in transform_tables()]
    features = jnp.asarray(position_features(band_rows // 2, length))

    (sent,) = call(
        pack_kernel, 10**9,
        [(NEAR, (side, channels, tokens + group), bf16)],
        [(out_weight.shape, bf16), (grad_out.shape, bf16)],
        2,
        (FAR, out_weight), (FAR, grad_out),
    )
    sent = exchange(sent, "ch", near_groups)
    cotangent = sent[:, :, :tokens].reshape(group, tokens)
    weight = sent[:, :, tokens:].reshape(group, group)
    grad_terms = lax.dot_general(
        weight, cotangent, (((0,), (0,)), ((), ())), preferred_element_type=f32
    ).astype(bf16)
    grad_terms = grad_terms.reshape(places, 2, channels, tokens)
    received = other_half(lax.dynamic_index_in_dim(grad_terms, 1 - half, 1, False))
    grad_terms = lax.dynamic_index_in_dim(grad_terms, half, 1, False)
    grad_terms = (grad_terms.astype(f32) + received.astype(f32)).astype(bf16)
    grad_terms = exchange(grad_terms, "ch", place_groups)
    grad_gated = jnp.sum(grad_terms.astype(f32), axis=0).astype(bf16)

    by_share = streams.reshape(3, blocks, share, tokens).transpose(1, 0, 2, 3)
    by_share = jnp.pad(by_share, ((0, 0), (0, 0), (0, pad_rows), (0, 0)))
    sequence = exchange(by_share.reshape(blocks, 3 * ROWS, tokens), "ctx")

    params = jnp.concatenate(
        [
            short_taps.transpose(1, 0, 2).reshape(channels, 9),
            decay_rate[:, None],
            skip_gain[:, None],
            filter_out.T,
        ],
        axis=1,
    )
    params = lax.dynamic_slice_in_dim(params, me * share, share, 0)
    params = jnp.pad(params, ((0, pad_rows), (0, 128 - params.shape[1])))

    def near(*values):
        return [(NEAR, value) for value in values]

    def far_like(shapes):
        return [(FAR,) + shape for shape in shapes]

    wave = ((hidden, length), f32)
    spectrum = ((blocks, ROWS, 2 * tokens), f32)
    kept_waves = [wave] * 4 + [spectrum]
    *waves, spectra = call(
        network_kernel, 4 * 10**9, far_like(kept_waves), kept_waves + [((blocks * ROWS, tokens), f32)], 5,
        *near(features, filter_in, filter_mid, params, tables[0], tables[1]),
    )
    kept = [
        ((blocks * ROWS, tokens), bf16),
        ((blocks, 3 * ROWS, tokens), f32),
        ((blocks, ROWS, tokens), f32),
        spectrum,
    ]
    gated, filtered, long_out, own_spectra = call(
        forward_kernel, 10**9, far_like(kept), kept + [((blocks * ROWS, 2 * tokens), f32)], 4,
        *near(sequence, params, spectra, *tables),
    )

    turned = jnp.pad(grad_gated.reshape(blocks, share, tokens), ((0, 0), (0, pad_rows), (0, 0)))
    turned = jnp.concatenate([gated.reshape(blocks, ROWS, tokens), turned], axis=1)
    turned = exchange(turned, "ctx")
    own_gated = turned[:, :share, :].reshape(channels, tokens)
    there_gated = other_half(own_gated)

    packed_streams = ((blocks, 6 * ROWS, tokens // 2), bf16)
    grad_packed, grad_shared, grad_last = call(
        backward_kernel, 4 * 10**9,
        [
            (FAR,) + packed_streams,
            (NEAR, (band_rows + hidden, hidden), bf16),
            (NEAR, (2 * ROWS, hidden), bf16),
        ],
        [spectrum, kept[1], kept[2], spectrum]
        + [wave] * 4
        + [packed_streams]
        + [((blocks * ROWS, 2 * tokens), f32)] * 2
        + [spectrum],
        9,
        *[(FAR, value) for value in (spectra, filtered, long_out, own_spectra, *waves)],
        *near(turned, params, features, filter_mid, *tables),
    )

    shared_rows = grad_shared.size // tokens
    sent = jnp.concatenate(
        [
            jnp.where(half == 0, own_gated, there_gated),
            jnp.where(half == 0, there_gated, own_gated),
            grad_shared.reshape(shared_rows, tokens),
        ],
        axis=0,
    )
    sent = exchange(
        jnp.broadcast_to(sent[None], (places,) + sent.shape), "ch", place_groups
    )
    all_gated = sent[:, : 2 * channels].reshape(group, tokens)
    shared = jnp.sum(sent[:, 2 * channels :].astype(f32), axis=0)

    out_terms = jnp.dot(weight, all_gated, preferred_element_type=f32).astype(bf16)
    def both_halves(value):
        high = lax.reduce_precision(value, 8, 7)
        return high.astype(bf16), (value - high).astype(bf16)

    chips = blocks // 2
    core = me % 2
    rows = side * share
    portion = (band_rows + hidden) // blocks
    by_core = cotangent.reshape(side, chips, 2, share, tokens).transpose(2, 1, 0, 3, 4)
    shared = shared.reshape(chips, 2, portion, hidden)
    grad_packed = grad_packed.reshape((chips, 2) + grad_packed.shape[1:])

    def parts_for(which):
        left = lax.dynamic_index_in_dim(by_core, which, 0, False).reshape(chips * rows, tokens)
        terms = lax.dot_general(
            left, all_gated, (((1,), (1,)), ((), ())), preferred_element_type=f32
        ).reshape(chips, rows, group)
        return (
            terms,
            lax.dynamic_index_in_dim(shared, which, 1, False),
            lax.dynamic_index_in_dim(grad_packed, which, 1, False),
        )

    def joined(terms, shared, lasts, packed):
        high, low = both_halves(shared)
        small = jnp.concatenate([high, low] + lasts, axis=1)
        small = jnp.pad(small, ((0, 0), (0, rows - small.shape[1]), (0, 0)))
        return jnp.concatenate([terms.astype(bf16), small] + packed, axis=2)

    last_here = jnp.broadcast_to(grad_last[None], (chips,) + grad_last.shape)
    terms, shared_part, packed = parts_for(1 - core)
    sent = joined(terms, shared_part, [last_here], [packed])
    core_pairs = [(k, k ^ 1) for k in range(blocks)]
    chip_groups = [[2 * z + c for z in range(chips)] for c in range(2)]
    sent = lax.ppermute(sent, "ctx", core_pairs)
    terms, shared_part, packed = parts_for(core)
    terms = terms + sent[:, :, :group].astype(f32)
    small = sent[:, :, group : group + hidden]
    shared_part = (
        shared_part
        + small[:, :portion].astype(f32)
        + small[:, portion : 2 * portion].astype(f32)
    )
    last_at = 2 * portion
    last_there = small[:, last_at : last_at + 2 * ROWS]
    packed_there = sent[:, :, group + hidden :]
    second = core == 1

    def in_order(here, there):
        return [jnp.where(second, there, here), jnp.where(second, here, there)]

    sent = joined(
        terms, shared_part, in_order(last_here, last_there), in_order(packed, packed_there)
    )
    sent = exchange(sent, "ctx", chip_groups)
    weight_share = jnp.sum(sent[:, :, :group].astype(f32), axis=0).astype(bf16)
    small = sent[:, :, group : group + hidden].astype(f32)
    shared = jnp.sum(small[:, :portion] + small[:, portion : 2 * portion], axis=0)
    shared = shared + other_half(shared)
    lasts = small[:, last_at : last_at + 4 * ROWS].reshape(blocks, 2, ROWS, hidden)[:, :, :share]
    grad_filter_out = jnp.sum(lasts, axis=1).reshape(channels, hidden).T
    packed = sent[:, :, group + hidden :].reshape(chips, 2, 3, ROWS, 2, tokens // 2)
    grad_streams = (
        packed[:, :, :, :share].transpose(2, 0, 4, 3, 1, 5).reshape(3, channels, tokens)
    )

    high, low = both_halves(shared)
    width = 3 * tokens
    tail = jnp.concatenate([high, low], axis=0).reshape(2 * portion * hidden // tokens, tokens)
    weight_rows = jnp.pad(
        weight_share.reshape(side, share, group), ((0, 0), (0, 0), (0, width - group))
    ).reshape(side, share * 3, tokens)
    sent = jnp.concatenate(
        [
            out_terms.reshape(side, channels, tokens),
            weight_rows,
            jnp.broadcast_to(tail[None], (side,) + tail.shape),
        ],
        axis=1,
    )
    sent = exchange(sent, "ch", near_groups)
    layer_out = jnp.sum(sent[:, :channels].astype(f32), axis=0).astype(bf16)
    weight_rows = sent[:, channels : channels + 3 * share].reshape(side, share, width)[:, :, :group]
    weight_rows = weight_rows.reshape(side, share, places, 2, channels).transpose(1, 3, 2, 0, 4)
    weight_rows = weight_rows.reshape(share, owners * channels)
    tail = jnp.sum(sent[:, channels + 3 * share :].astype(f32), axis=0)
    tail = tail.reshape(2, portion * hidden)
    high, low = both_halves(tail[0] + tail[1])

    tail = jnp.concatenate([high, low])
    spare = -tail.size % (share * 128)
    tail = jnp.pad(tail, (0, spare)).reshape(share, -1)
    sent = jnp.concatenate([weight_rows, tail], axis=1)
    here = lax.all_gather(sent, "ctx", axis=0, axis_index_groups=chip_groups)
    there = lax.ppermute(here, "ctx", core_pairs)
    sent = jnp.stack(in_order(here, there), axis=1).reshape(blocks, share, -1)
    grad_out_weight = sent[:, :, : weight_rows.shape[1]].reshape(channels, -1).astype(f32)
    tail = sent[:, :, weight_rows.shape[1] :].reshape(blocks, -1).astype(f32)
    size = portion * hidden
    shared = (tail[:, :size] + tail[:, size : 2 * size]).reshape(band_rows + hidden, hidden)
    return (
        layer_out, grad_streams, shared[:band_rows], shared[band_rows:], grad_filter_out,
        grad_out_weight,
    )


def solution(mesh):
    return jax.shard_map(
        shards,
        mesh=mesh,
        in_specs=(
            P(None, "ch", "ctx"),
            P(None, "ch", None),
            P(),
            P(),
            P(None, "ch"),
            P("ch"),
            P("ch"),
            P("ch", None),
            P("ch", "ctx"),
        ),
        out_specs=(P("ch", "ctx"), P(None, "ch", "ctx"), P(), P(), P(None, "ch"), P("ch", None)),
        check_vma=False,
    )
```

```python
import functools
import math

import jax
import jax.numpy as jnp
import numpy as np
from jax import lax
from jax.experimental import pallas as pl
from jax.experimental.pallas import tpu as pltpu
from jax.sharding import PartitionSpec as P

f32 = jnp.float32
bf16 = jnp.bfloat16

BLOCK = 256
ROWS = 8
VMEM_LIMIT = 16 * 1024 * 1024


def split_table(table):
    high = table.astype(np.float32).astype(jnp.bfloat16)
    low = (table - high.astype(np.float64)).astype(np.float32).astype(jnp.bfloat16)
    return high, low


@functools.lru_cache(maxsize=None)
def transform_tables():
    frequency = np.arange(BLOCK)
    token = np.arange(BLOCK)
    angle = np.pi * ((2 * frequency[None, :] + 1) * token[:, None] % (4 * BLOCK)) / (2 * BLOCK)
    forward = np.concatenate([np.cos(angle), -np.sin(angle)], axis=1)
    return split_table(forward) + split_table(forward.T / BLOCK)


@functools.lru_cache(maxsize=None)
def position_features(band_count, length):
    wrapped = (np.arange(1, band_count + 1)[:, None] * np.arange(length)[None, :]) % length
    phases = 2.0 * np.pi / length * wrapped
    return np.concatenate([np.cos(phases), np.sin(phases)], axis=0).astype(np.float32)


def halves(value):
    high = value.astype(bf16)
    return high, (value - high.astype(f32)).astype(bf16)


def plain_dot(left, right, dims):
    return lax.dot_general(left, right, (dims, ((), ())), preferred_element_type=f32)


def close_dot(left, right, dims=((1,), (0,))):
    left_high, left_low = halves(left)
    right_high, right_low = halves(right)
    return (
        plain_dot(left_high, right_high, dims)
        + plain_dot(left_high, right_low, dims)
        + plain_dot(left_low, right_high, dims)
    )


def table_dot(left, high, low):
    dims = ((1,), (0,))
    if left.dtype == bf16:
        return plain_dot(left, high, dims) + plain_dot(left, low, dims)
    left_high, left_low = halves(left)
    return (
        plain_dot(left_high, high, dims)
        + plain_dot(left_high, low, dims)
        + plain_dot(left_low, high, dims)
    )


def sine_and_cosine(value):
    turns = jnp.floor(value * (2.0 / math.pi) + 0.5)
    rest = value - turns * 1.5703125
    rest = rest - turns * 4.837512969970703125e-4
    rest = rest - turns * 7.54978994876864e-8
    square = rest * rest
    sine = rest + rest * square * (
        -1.6666654611e-1 + square * (8.3321608736e-3 + square * -1.9515295891e-4)
    )
    cosine = (
        1.0
        - 0.5 * square
        + square
        * square
        * (4.166664568298827e-2 + square * (-1.388731625493765e-3 + square * 2.443315711809948e-5))
    )
    quadrant = turns.astype(jnp.int32)
    odd = (quadrant & 1) == 1
    sine_out = jnp.where(odd, cosine, sine)
    cosine_out = jnp.where(odd, sine, cosine)
    sine_out = jnp.where((quadrant & 2) == 2, -sine_out, sine_out)
    cosine_out = jnp.where(((quadrant + 1) & 2) == 2, -cosine_out, cosine_out)
    return sine_out, cosine_out


def envelope(decay, block):
    lag = (lax.broadcasted_iota(jnp.int32, (ROWS, BLOCK), 1) + block * BLOCK).astype(f32)
    return jnp.exp(-decay * lag) * jnp.sqrt(decay)


def parity():
    odd = lax.broadcasted_iota(jnp.int32, (ROWS, BLOCK), 1) & 1
    return (1 - 2 * odd).astype(f32)


DECAY, SKIP, OUT = 9, 10, 11


def start_copies(pairs, semaphores):
    copies = [
        pltpu.make_async_copy(source, target, semaphores.at[i])
        for i, (source, target) in enumerate(pairs)
    ]
    for copy in copies:
        copy.start()
    return copies


def wait_copies(copies):
    for copy in copies:
        copy.wait()


def network_kernel(
    features, filter_in, filter_mid, params, table_high, table_low,
    kept_one, kept_slope_one, kept_two, kept_slope_two, kept_spectra,
    hidden_one, slope_one, hidden_two, slope_two, spectra, taps_scratch, semaphores,
):
    count = features.shape[1] // BLOCK
    hidden = filter_in.shape[1]
    decay = params[:, DECAY : DECAY + 1]
    last = params[:, OUT : OUT + hidden]
    for block in range(count):
        at = slice(block * BLOCK, (block + 1) * BLOCK)
        sine, cosine = sine_and_cosine(
            close_dot(filter_in[...], features[:, at], ((0,), (0,)))
        )
        hidden_one[:, at] = sine
        slope_one[:, at] = cosine
        sine, cosine = sine_and_cosine(close_dot(filter_mid[...], sine, ((0,), (0,))))
        hidden_two[:, at] = sine
        slope_two[:, at] = cosine
        raw = close_dot(last, sine)
        taps_scratch[block * ROWS : (block + 1) * ROWS, :] = raw * envelope(decay, block)
    copies = start_copies(
        [
            (hidden_one, kept_one),
            (slope_one, kept_slope_one),
            (hidden_two, kept_two),
            (slope_two, kept_slope_two),
        ],
        semaphores,
    )
    spectrum = table_dot(taps_scratch[...], table_high[...], table_low[...])
    sign = parity()
    for block in range(count):
        real = spectrum[block * ROWS : (block + 1) * ROWS, :BLOCK]
        imag = spectrum[block * ROWS : (block + 1) * ROWS, BLOCK:]
        if block:
            before = slice((block - 1) * ROWS, block * ROWS)
            real = real - sign * spectrum[before, BLOCK:]
            imag = imag + sign * spectrum[before, :BLOCK]
        spectra[block, :, :BLOCK] = real
        spectra[block, :, BLOCK:] = imag
    last_copy = pltpu.make_async_copy(spectra, kept_spectra, semaphores.at[4])
    last_copy.start()
    wait_copies(copies + [last_copy])


def rows_of(value, rows):
    return value.reshape(value.shape[0] // rows, rows, value.shape[1])


def forward_kernel(
    blocks, params, spectra, table_high, table_low, back_high, back_low,
    kept_gated, kept_filtered, kept_long_out, kept_spectra,
    gated, filtered, long_out, own_spectra, sums, semaphores,
):
    count = blocks.shape[0]
    wide = 3 * ROWS
    raw = blocks[...].astype(f32).reshape(count * wide, BLOCK)
    lane = lax.broadcasted_iota(jnp.int32, (count * wide, BLOCK), 1)
    lead = jnp.zeros((wide, BLOCK), f32)
    shifted = [raw]
    for by in (1, 2):
        rolled = pltpu.roll(raw, by, 1)
        before = jnp.concatenate([lead, rolled[:-wide]], axis=0)
        shifted.append(jnp.where(lane < by, before, rolled))
    shifted = [rows_of(value, wide) for value in shifted]
    streams = []
    for stream in range(3):
        at = slice(stream * ROWS, (stream + 1) * ROWS)
        total = None
        for tap in range(3):
            column = stream * 3 + tap
            term = params[:, column : column + 1][None] * shifted[tap][:, at, :]
            total = term if total is None else total + term
        filtered[:, at, :] = total
        streams.append(total)
    product = (streams[1] * streams[2]).astype(bf16).astype(f32).reshape(count * ROWS, BLOCK)
    spectrum = table_dot(product.astype(bf16), table_high[...], table_low[...])
    own_spectra[...] = rows_of(spectrum, ROWS)
    for block in range(count):
        real = jnp.zeros((ROWS, BLOCK), f32)
        imag = jnp.zeros((ROWS, BLOCK), f32)
        for source in range(block + 1):
            filter_real = spectra[block - source, :, :BLOCK]
            filter_imag = spectra[block - source, :, BLOCK:]
            own_real = own_spectra[source, :, :BLOCK]
            own_imag = own_spectra[source, :, BLOCK:]
            real = real + filter_real * own_real - filter_imag * own_imag
            imag = imag + filter_real * own_imag + filter_imag * own_real
        sums[block * ROWS : (block + 1) * ROWS, :BLOCK] = real
        sums[block * ROWS : (block + 1) * ROWS, BLOCK:] = imag
    conv = table_dot(sums[...], back_high[...], back_low[...])
    skip = params[:, SKIP : SKIP + 1][None]
    result = rows_of(conv, ROWS) + skip * rows_of(product, ROWS)
    long_out[...] = result
    gated[...] = (streams[0] * result).reshape(count * ROWS, BLOCK).astype(bf16)
    wait_copies(
        start_copies(
            [
                (gated, kept_gated),
                (filtered, kept_filtered),
                (long_out, kept_long_out),
                (own_spectra, kept_spectra),
            ],
            semaphores,
        )
    )


def backward_kernel(
    kept_spectra, kept_filtered, kept_long_out, kept_own_spectra,
    kept_one, kept_slope_one, kept_two, kept_slope_two,
    blocks, params, features, filter_mid, table_high, table_low, back_high, back_low,
    kept_grad_streams, grad_shared, grad_last,
    spectra, filtered, long_out, own_spectra, hidden_one, slope_one, hidden_two, slope_two,
    grad_streams, sums, lag_sums, grad_spectra, semaphores,
):
    copies = start_copies(
        [
            (kept_filtered, filtered),
            (kept_spectra, spectra),
            (kept_own_spectra, own_spectra),
            (kept_long_out, long_out),
            (kept_two, hidden_two),
            (kept_slope_two, slope_two),
            (kept_one, hidden_one),
            (kept_slope_one, slope_one),
        ],
        semaphores,
    )
    count = blocks.shape[0]
    hidden = filter_mid.shape[0]
    wide = 3 * ROWS
    grad_gated = blocks[...].astype(f32)[:, ROWS : 2 * ROWS, :]
    wait_copies(copies[:4])
    query = filtered[:, :ROWS, :]
    grad_long = (grad_gated * query).reshape(count * ROWS, BLOCK).astype(bf16)
    spectrum = table_dot(grad_long, table_high[...], table_low[...])
    grad_spectra[...] = rows_of(spectrum, ROWS)
    sign = parity()
    after = None
    for block in reversed(range(count)):
        back_real = jnp.zeros((ROWS, BLOCK), f32)
        back_imag = jnp.zeros((ROWS, BLOCK), f32)
        lag_real = jnp.zeros((ROWS, BLOCK), f32)
        lag_imag = jnp.zeros((ROWS, BLOCK), f32)
        for target in range(block, count):
            grad_real = grad_spectra[target, :, :BLOCK]
            grad_imag = grad_spectra[target, :, BLOCK:]
            filter_real = spectra[target - block, :, :BLOCK]
            filter_imag = spectra[target - block, :, BLOCK:]
            back_real = back_real + filter_real * grad_real + filter_imag * grad_imag
            back_imag = back_imag + filter_real * grad_imag - filter_imag * grad_real
            own_real = own_spectra[target - block, :, :BLOCK]
            own_imag = own_spectra[target - block, :, BLOCK:]
            lag_real = lag_real + own_real * grad_real + own_imag * grad_imag
            lag_imag = lag_imag + own_real * grad_imag - own_imag * grad_real
        at = slice(block * ROWS, (block + 1) * ROWS)
        sums[at, :BLOCK] = back_real
        sums[at, BLOCK:] = back_imag
        if after is None:
            lag_sums[at, :BLOCK] = lag_real
            lag_sums[at, BLOCK:] = lag_imag
        else:
            lag_sums[at, :BLOCK] = lag_real + sign * after[1]
            lag_sums[at, BLOCK:] = lag_imag - sign * after[0]
        after = (lag_real, lag_imag)
    back = table_dot(sums[...], back_high[...], back_low[...])
    skip = params[:, SKIP : SKIP + 1][None]
    grad_product = rows_of(back, ROWS) + skip * rows_of(grad_long.astype(f32), ROWS)
    grads = [
        grad_gated * long_out[...],
        grad_product * filtered[:, 2 * ROWS :, :],
        grad_product * filtered[:, ROWS : 2 * ROWS, :],
    ]
    lane = lax.broadcasted_iota(jnp.int32, (count * ROWS, BLOCK), 1)
    tail = jnp.zeros((ROWS, BLOCK), f32)
    adjoint = []
    for stream in range(3):
        value = grads[stream].reshape(count * ROWS, BLOCK)
        total = params[:, stream * 3 : stream * 3 + 1][None] * grads[stream]
        for by in (1, 2):
            rolled = pltpu.roll(value, BLOCK - by, 1)
            following = jnp.concatenate([rolled[ROWS:], tail], axis=0)
            moved = jnp.where(lane >= BLOCK - by, following, rolled)
            column = stream * 3 + by
            total = total + params[:, column : column + 1][None] * rows_of(moved, ROWS)
        adjoint.append(total)
    half = BLOCK // 2
    packed = [part[:, :, :half] for part in adjoint] + [part[:, :, half:] for part in adjoint]
    grad_streams[...] = jnp.concatenate(packed, axis=1).astype(bf16)
    streams_copy = pltpu.make_async_copy(grad_streams, kept_grad_streams, semaphores.at[8])
    streams_copy.start()
    wait_copies(copies[4:])

    lags = table_dot(lag_sums[...], back_high[...], back_low[...])
    decay = params[:, DECAY : DECAY + 1]
    last = params[:, OUT : OUT + hidden]
    raw = [
        lags[block * ROWS : (block + 1) * ROWS] * envelope(decay, block)
        for block in range(count)
    ]
    total_last = jnp.zeros((ROWS, hidden), f32)
    total_mid = jnp.zeros((hidden, hidden), f32)
    total_in = jnp.zeros((features.shape[0], hidden), f32)
    across = ((1,), (1,))
    for block in range(count):
        at = slice(block * BLOCK, (block + 1) * BLOCK)
        total_last = total_last + close_dot(raw[block], hidden_two[:, at], across)
        grad_two = close_dot(last, raw[block], ((0,), (0,))) * slope_two[:, at]
        total_mid = total_mid + close_dot(hidden_one[:, at], grad_two, across)
        grad_one = close_dot(filter_mid[...], grad_two) * slope_one[:, at]
        total_in = total_in + close_dot(features[:, at], grad_one, across)
    grad_shared[...] = jnp.concatenate([total_in, total_mid], axis=0).astype(bf16)
    high, low = halves(total_last)
    grad_last[...] = jnp.concatenate([high.astype(f32), low.astype(f32)], axis=0).astype(bf16)
    streams_copy.wait()


def pack_kernel(far_weight, far_cotangent, packed, weight, cotangent, semaphores):
    wait_copies(
        start_copies([(far_weight, weight), (far_cotangent, cotangent)], semaphores)
    )
    side = packed.shape[0]
    channels, tokens = cotangent.shape
    for i in range(side):
        packed[i, :, :tokens] = cotangent[...]
        pieces = [
            weight[:, (a * side + i) * channels : (a * side + i + 1) * channels]
            for a in range(side)
        ]
        packed[i, :, tokens:] = jnp.concatenate(pieces, axis=1)


NEAR, FAR = pltpu.VMEM, pltpu.HBM


def call(kernel, outs, scratch, copies, *operands):
    semaphores = [pltpu.SemaphoreType.DMA((copies,))] if copies else []
    return pl.pallas_call(
        kernel,
        out_shape=[
            pltpu.HBM(shape, kind) if place is FAR else jax.ShapeDtypeStruct(shape, kind)
            for place, shape, kind in outs
        ],
        in_specs=[pl.BlockSpec(memory_space=place) for place, _ in operands],
        out_specs=[pl.BlockSpec(memory_space=place) for place, _, _ in outs],
        scratch_shapes=[pltpu.VMEM(shape, kind) for shape, kind in scratch] + semaphores,
        compiler_params=pltpu.CompilerParams(vmem_limit_bytes=VMEM_LIMIT),
    )(
        *[
            pltpu.with_memory_space_constraint(operand, FAR) if place is FAR else operand
            for place, operand in operands
        ]
    )


def exchange(value, axis, groups=None):
    return lax.all_to_all(value, axis, 0, 0, tiled=True, axis_index_groups=groups)


def shards(
    streams, short_taps, filter_in, filter_mid, filter_out, decay_rate, skip_gain, out_weight,
    grad_out,
):
    channels, tokens = streams.shape[1:]
    blocks = lax.axis_size("ctx")
    owners = lax.axis_size("ch")
    me = lax.axis_index("ctx")
    length = blocks * tokens
    share = channels // blocks
    hidden = filter_in.shape[1]
    band_rows = filter_in.shape[0]
    side = int(math.isqrt(owners))
    near_groups = [[a * side + i for i in range(side)] for a in range(side)]
    far_groups = [[a * side + i for a in range(side)] for i in range(side)]
    places = side // 2
    place_groups = [group[h * places : (h + 1) * places] for group in far_groups for h in range(2)]
    half = lax.axis_index("ch") // (places * side)
    group = side * channels
    pad_rows = ROWS - share
    tables = [jnp.asarray(t) for t in transform_tables()]
    features = jnp.asarray(position_features(band_rows // 2, length))

    (sent,) = call(
        pack_kernel,
        [(NEAR, (side, channels, tokens + group), bf16)],
        [(out_weight.shape, bf16), (grad_out.shape, bf16)],
        2,
        (FAR, out_weight), (FAR, grad_out),
    )
    sent = exchange(sent, "ch", near_groups)
    cotangent = sent[:, :, :tokens].reshape(group, tokens)
    weight = sent[:, :, tokens:].reshape(group, group)
    grad_terms = lax.dot_general(
        weight, cotangent, (((0,), (0,)), ((), ())), preferred_element_type=f32
    ).astype(bf16)
    grad_terms = grad_terms.reshape(2, places, channels, tokens)
    received = lax.ppermute(
        lax.dynamic_index_in_dim(grad_terms, 1 - half, 0, False),
        "ch",
        [(j, (j + places * side) % owners) for j in range(owners)],
    )
    grad_terms = lax.dynamic_index_in_dim(grad_terms, half, 0, False)
    grad_terms = (grad_terms.astype(f32) + received.astype(f32)).astype(bf16)
    grad_terms = exchange(grad_terms, "ch", place_groups)
    grad_gated = jnp.sum(grad_terms.astype(f32), axis=0).astype(bf16)

    params = jnp.concatenate(
        [
            short_taps.transpose(1, 0, 2).reshape(channels, 9),
            decay_rate[:, None],
            skip_gain[:, None],
            filter_out.T,
        ],
        axis=1,
    )
    params = lax.dynamic_slice_in_dim(params, me * share, share, 0)
    params = jnp.pad(params, ((0, pad_rows), (0, 128 - params.shape[1])))

    def near(*values):
        return [(NEAR, value) for value in values]

    def far_like(shapes):
        return [(FAR,) + shape for shape in shapes]

    wave = ((hidden, length), f32)
    spectrum = ((blocks, ROWS, 2 * tokens), f32)
    kept_waves = [wave] * 4 + [spectrum]
    *waves, spectra = call(
        network_kernel, far_like(kept_waves), kept_waves + [((blocks * ROWS, tokens), f32)], 5,
        *near(features, filter_in, filter_mid, params, tables[0], tables[1]),
    )

    by_share = streams.reshape(3, blocks, share, tokens).transpose(1, 0, 2, 3)
    by_share = jnp.pad(by_share, ((0, 0), (0, 0), (0, pad_rows), (0, 0)))
    by_share, spectra = lax.optimization_barrier((by_share, spectra))
    sequence = exchange(by_share.reshape(blocks, 3 * ROWS, tokens), "ctx")
    kept = [
        ((blocks * ROWS, tokens), bf16),
        ((blocks, 3 * ROWS, tokens), f32),
        ((blocks, ROWS, tokens), f32),
        spectrum,
    ]
    gated, filtered, long_out, own_spectra = call(
        forward_kernel, far_like(kept), kept + [((blocks * ROWS, 2 * tokens), f32)], 4,
        *near(sequence, params, spectra, *tables),
    )

    turned = jnp.pad(grad_gated.reshape(blocks, share, tokens), ((0, 0), (0, pad_rows), (0, 0)))
    turned = jnp.concatenate([gated.reshape(blocks, ROWS, tokens), turned], axis=1)
    turned = exchange(turned, "ctx")
    own_gated = turned[:, :share, :].reshape(channels, tokens)

    packed_streams = ((blocks, 6 * ROWS, tokens // 2), bf16)
    grad_packed, grad_shared, grad_last = call(
        backward_kernel,
        [
            (FAR,) + packed_streams,
            (NEAR, (band_rows + hidden, hidden), bf16),
            (NEAR, (2 * ROWS, hidden), bf16),
        ],
        [spectrum, kept[1], kept[2], spectrum]
        + [wave] * 4
        + [packed_streams]
        + [((blocks * ROWS, 2 * tokens), f32)] * 2
        + [spectrum],
        9,
        *[(FAR, value) for value in (spectra, filtered, long_out, own_spectra, *waves)],
        *near(turned, params, features, filter_mid, *tables),
    )

    shared_rows = grad_shared.size // tokens
    sent = jnp.concatenate([own_gated, grad_shared.reshape(shared_rows, tokens)], axis=0)
    sent = exchange(
        jnp.broadcast_to(sent[None], (side,) + sent.shape), "ch", far_groups
    )
    all_gated = sent[:, :channels].reshape(group, tokens)
    shared = jnp.sum(sent[:, channels:].astype(f32), axis=0)

    out_terms = jnp.dot(weight, all_gated, preferred_element_type=f32).astype(bf16)
    def both_halves(value):
        high = lax.reduce_precision(value, 8, 7)
        return high.astype(bf16), (value - high).astype(bf16)

    chips = blocks // 2
    core = me % 2
    rows = side * share
    portion = (band_rows + hidden) // blocks
    by_core = cotangent.reshape(side, chips, 2, share, tokens).transpose(2, 1, 0, 3, 4)
    shared = shared.reshape(chips, 2, portion, hidden)
    grad_packed = grad_packed.reshape((chips, 2) + grad_packed.shape[1:])

    def parts_for(which):
        left = lax.dynamic_index_in_dim(by_core, which, 0, False).reshape(chips * rows, tokens)
        terms = lax.dot_general(
            left, all_gated, (((1,), (1,)), ((), ())), preferred_element_type=f32
        ).reshape(chips, rows, group)
        return (
            terms,
            lax.dynamic_index_in_dim(shared, which, 1, False),
            lax.dynamic_index_in_dim(grad_packed, which, 1, False),
        )

    def joined(terms, shared, lasts, packed):
        high, low = both_halves(shared)
        small = jnp.concatenate([high, low] + lasts, axis=1)
        small = jnp.pad(small, ((0, 0), (0, rows - small.shape[1]), (0, 0)))
        return jnp.concatenate([terms.astype(bf16), small] + packed, axis=2)

    last_here = jnp.broadcast_to(grad_last[None], (chips,) + grad_last.shape)
    terms, shared_part, packed = parts_for(1 - core)
    sent = joined(terms, shared_part, [last_here], [packed])
    sent = lax.ppermute(sent, "ctx", [(k, k ^ 1) for k in range(blocks)])
    terms, shared_part, packed = parts_for(core)
    terms = terms + sent[:, :, :group].astype(f32)
    small = sent[:, :, group : group + hidden]
    shared_part = (
        shared_part
        + small[:, :portion].astype(f32)
        + small[:, portion : 2 * portion].astype(f32)
    )
    last_at = 2 * portion
    last_there = small[:, last_at : last_at + 2 * ROWS]
    packed_there = sent[:, :, group + hidden :]
    second = core == 1

    def in_order(here, there):
        return [jnp.where(second, there, here), jnp.where(second, here, there)]

    sent = joined(
        terms, shared_part, in_order(last_here, last_there), in_order(packed, packed_there)
    )
    sent = exchange(sent, "ctx", [[2 * z + c for z in range(chips)] for c in range(2)])
    weight_share = jnp.sum(sent[:, :, :group].astype(f32), axis=0).astype(bf16)
    small = sent[:, :, group : group + hidden].astype(f32)
    shared = jnp.sum(small[:, :portion] + small[:, portion : 2 * portion], axis=0)
    lasts = small[:, last_at : last_at + 4 * ROWS].reshape(blocks, 2, ROWS, hidden)[:, :, :share]
    grad_filter_out = jnp.sum(lasts, axis=1).reshape(channels, hidden).T
    packed = sent[:, :, group + hidden :].reshape(chips, 2, 3, ROWS, 2, tokens // 2)
    grad_streams = (
        packed[:, :, :, :share].transpose(2, 0, 4, 3, 1, 5).reshape(3, channels, tokens)
    )

    high, low = both_halves(shared)
    width = 3 * tokens
    tail = jnp.concatenate([high, low], axis=0).reshape(2 * portion * hidden // tokens, tokens)
    weight_rows = jnp.pad(
        weight_share.reshape(side, share, group), ((0, 0), (0, 0), (0, width - group))
    ).reshape(side, share * 3, tokens)
    sent = jnp.concatenate(
        [
            out_terms.reshape(side, channels, tokens),
            weight_rows,
            jnp.broadcast_to(tail[None], (side,) + tail.shape),
        ],
        axis=1,
    )
    sent = exchange(sent, "ch", near_groups)
    layer_out = jnp.sum(sent[:, :channels].astype(f32), axis=0).astype(bf16)
    weight_rows = sent[:, channels : channels + 3 * share].reshape(side, share, width)[:, :, :group]
    weight_rows = weight_rows.reshape(side, share, side, channels).transpose(1, 2, 0, 3)
    weight_rows = weight_rows.reshape(share, owners * channels)
    tail = jnp.sum(sent[:, channels + 3 * share :].astype(f32), axis=0)
    tail = tail.reshape(2, portion * hidden)
    high, low = both_halves(tail[0] + tail[1])

    tail = jnp.concatenate([high, low])
    spare = -tail.size % (share * 128)
    tail = jnp.pad(tail, (0, spare)).reshape(share, -1)
    sent = lax.all_gather(jnp.concatenate([weight_rows, tail], axis=1), "ctx", axis=0)
    grad_out_weight = sent[:, :, : weight_rows.shape[1]].reshape(channels, -1).astype(f32)
    tail = sent[:, :, weight_rows.shape[1] :].reshape(blocks, -1).astype(f32)
    size = portion * hidden
    shared = (tail[:, :size] + tail[:, size : 2 * size]).reshape(band_rows + hidden, hidden)
    return (
        layer_out, grad_streams, shared[:band_rows], shared[band_rows:], grad_filter_out,
        grad_out_weight,
    )


def solution(mesh):
    return jax.shard_map(
        shards,
        mesh=mesh,
        in_specs=(
            P(None, "ch", "ctx"),
            P(None, "ch", None),
            P(),
            P(),
            P(None, "ch"),
            P("ch"),
            P("ch"),
            P("ch", None),
            P("ch", "ctx"),
        ),
        out_specs=(P("ch", "ctx"), P(None, "ch", "ctx"), P(), P(), P(None, "ch"), P("ch", None)),
        check_vma=False,
    )
```

```python
import functools
import math

import jax
import jax.numpy as jnp
import numpy as np
from jax import lax
from jax.experimental import pallas as pl
from jax.experimental.pallas import tpu as pltpu
from jax.sharding import PartitionSpec as P

f32 = jnp.float32
bf16 = jnp.bfloat16

BLOCK = 256
ROWS = 8
VMEM_LIMIT = 16 * 1024 * 1024


def split_table(table):
    high = table.astype(np.float32).astype(jnp.bfloat16)
    low = (table - high.astype(np.float64)).astype(np.float32).astype(jnp.bfloat16)
    return high, low


@functools.lru_cache(maxsize=None)
def transform_tables():
    frequency = np.arange(BLOCK)
    token = np.arange(BLOCK)
    angle = np.pi * ((2 * frequency[None, :] + 1) * token[:, None] % (4 * BLOCK)) / (2 * BLOCK)
    forward = np.concatenate([np.cos(angle), -np.sin(angle)], axis=1)
    return split_table(forward) + split_table(forward.T / BLOCK)


@functools.lru_cache(maxsize=None)
def position_features(band_count, length):
    wrapped = (np.arange(1, band_count + 1)[:, None] * np.arange(length)[None, :]) % length
    phases = 2.0 * np.pi / length * wrapped
    return np.concatenate([np.cos(phases), np.sin(phases)], axis=0).astype(np.float32)


def halves(value):
    high = value.astype(bf16)
    return high, (value - high.astype(f32)).astype(bf16)


def plain_dot(left, right, dims):
    return lax.dot_general(left, right, (dims, ((), ())), preferred_element_type=f32)


def close_dot(left, right, dims=((1,), (0,))):
    left_high, left_low = halves(left)
    right_high, right_low = halves(right)
    return (
        plain_dot(left_high, right_high, dims)
        + plain_dot(left_high, right_low, dims)
        + plain_dot(left_low, right_high, dims)
    )


def table_dot(left, high, low):
    dims = ((1,), (0,))
    if left.dtype == bf16:
        return plain_dot(left, high, dims) + plain_dot(left, low, dims)
    left_high, left_low = halves(left)
    return (
        plain_dot(left_high, high, dims)
        + plain_dot(left_high, low, dims)
        + plain_dot(left_low, high, dims)
    )


def sine_and_cosine(value):
    turns = jnp.floor(value * (2.0 / math.pi) + 0.5)
    rest = value - turns * 1.5703125
    rest = rest - turns * 4.837512969970703125e-4
    rest = rest - turns * 7.54978994876864e-8
    square = rest * rest
    sine = rest + rest * square * (
        -1.6666654611e-1 + square * (8.3321608736e-3 + square * -1.9515295891e-4)
    )
    cosine = (
        1.0
        - 0.5 * square
        + square
        * square
        * (4.166664568298827e-2 + square * (-1.388731625493765e-3 + square * 2.443315711809948e-5))
    )
    quadrant = turns.astype(jnp.int32)
    odd = (quadrant & 1) == 1
    sine_out = jnp.where(odd, cosine, sine)
    cosine_out = jnp.where(odd, sine, cosine)
    sine_out = jnp.where((quadrant & 2) == 2, -sine_out, sine_out)
    cosine_out = jnp.where(((quadrant + 1) & 2) == 2, -cosine_out, cosine_out)
    return sine_out, cosine_out


def envelope(decay, block):
    lag = (lax.broadcasted_iota(jnp.int32, (ROWS, BLOCK), 1) + block * BLOCK).astype(f32)
    return jnp.exp(-decay * lag) * jnp.sqrt(decay)


def parity():
    odd = lax.broadcasted_iota(jnp.int32, (ROWS, BLOCK), 1) & 1
    return (1 - 2 * odd).astype(f32)


DECAY, SKIP, OUT = 9, 10, 11


def start_copies(pairs, semaphores):
    copies = [
        pltpu.make_async_copy(source, target, semaphores.at[i])
        for i, (source, target) in enumerate(pairs)
    ]
    for copy in copies:
        copy.start()
    return copies


def wait_copies(copies):
    for copy in copies:
        copy.wait()


def network_kernel(
    features, filter_in, filter_mid, params, table_high, table_low,
    kept_one, kept_slope_one, kept_two, kept_slope_two, kept_spectra,
    hidden_one, slope_one, hidden_two, slope_two, spectra, taps_scratch, semaphores,
):
    count = features.shape[1] // BLOCK
    hidden = filter_in.shape[1]
    decay = params[:, DECAY : DECAY + 1]
    last = params[:, OUT : OUT + hidden]
    for block in range(count):
        at = slice(block * BLOCK, (block + 1) * BLOCK)
        sine, cosine = sine_and_cosine(
            close_dot(filter_in[...], features[:, at], ((0,), (0,)))
        )
        hidden_one[:, at] = sine
        slope_one[:, at] = cosine
        sine, cosine = sine_and_cosine(close_dot(filter_mid[...], sine, ((0,), (0,))))
        hidden_two[:, at] = sine
        slope_two[:, at] = cosine
        raw = close_dot(last, sine)
        taps_scratch[block * ROWS : (block + 1) * ROWS, :] = raw * envelope(decay, block)
    copies = start_copies(
        [
            (hidden_one, kept_one),
            (slope_one, kept_slope_one),
            (hidden_two, kept_two),
            (slope_two, kept_slope_two),
        ],
        semaphores,
    )
    spectrum = table_dot(taps_scratch[...], table_high[...], table_low[...])
    sign = parity()
    for block in range(count):
        real = spectrum[block * ROWS : (block + 1) * ROWS, :BLOCK]
        imag = spectrum[block * ROWS : (block + 1) * ROWS, BLOCK:]
        if block:
            before = slice((block - 1) * ROWS, block * ROWS)
            real = real - sign * spectrum[before, BLOCK:]
            imag = imag + sign * spectrum[before, :BLOCK]
        spectra[block, :, :BLOCK] = real
        spectra[block, :, BLOCK:] = imag
    last_copy = pltpu.make_async_copy(spectra, kept_spectra, semaphores.at[4])
    last_copy.start()
    wait_copies(copies + [last_copy])


def rows_of(value, rows):
    return value.reshape(value.shape[0] // rows, rows, value.shape[1])


def forward_kernel(
    blocks, params, spectra, table_high, table_low, back_high, back_low,
    kept_gated, kept_filtered, kept_long_out, kept_spectra,
    gated, filtered, long_out, own_spectra, sums, semaphores,
):
    count = blocks.shape[0]
    wide = 3 * ROWS
    raw = blocks[...].astype(f32).reshape(count * wide, BLOCK)
    lane = lax.broadcasted_iota(jnp.int32, (count * wide, BLOCK), 1)
    lead = jnp.zeros((wide, BLOCK), f32)
    shifted = [raw]
    for by in (1, 2):
        rolled = pltpu.roll(raw, by, 1)
        before = jnp.concatenate([lead, rolled[:-wide]], axis=0)
        shifted.append(jnp.where(lane < by, before, rolled))
    shifted = [rows_of(value, wide) for value in shifted]
    streams = []
    for stream in range(3):
        at = slice(stream * ROWS, (stream + 1) * ROWS)
        total = None
        for tap in range(3):
            column = stream * 3 + tap
            term = params[:, column : column + 1][None] * shifted[tap][:, at, :]
            total = term if total is None else total + term
        filtered[:, at, :] = total
        streams.append(total)
    product = (streams[1] * streams[2]).astype(bf16).astype(f32).reshape(count * ROWS, BLOCK)
    spectrum = table_dot(product.astype(bf16), table_high[...], table_low[...])
    own_spectra[...] = rows_of(spectrum, ROWS)
    for block in range(count):
        real = jnp.zeros((ROWS, BLOCK), f32)
        imag = jnp.zeros((ROWS, BLOCK), f32)
        for source in range(block + 1):
            filter_real = spectra[block - source, :, :BLOCK]
            filter_imag = spectra[block - source, :, BLOCK:]
            own_real = own_spectra[source, :, :BLOCK]
            own_imag = own_spectra[source, :, BLOCK:]
            real = real + filter_real * own_real - filter_imag * own_imag
            imag = imag + filter_real * own_imag + filter_imag * own_real
        sums[block * ROWS : (block + 1) * ROWS, :BLOCK] = real
        sums[block * ROWS : (block + 1) * ROWS, BLOCK:] = imag
    conv = table_dot(sums[...], back_high[...], back_low[...])
    skip = params[:, SKIP : SKIP + 1][None]
    result = rows_of(conv, ROWS) + skip * rows_of(product, ROWS)
    long_out[...] = result
    gated[...] = (streams[0] * result).reshape(count * ROWS, BLOCK).astype(bf16)
    wait_copies(
        start_copies(
            [
                (gated, kept_gated),
                (filtered, kept_filtered),
                (long_out, kept_long_out),
                (own_spectra, kept_spectra),
            ],
            semaphores,
        )
    )


def backward_kernel(
    kept_spectra, kept_filtered, kept_long_out, kept_own_spectra,
    kept_one, kept_slope_one, kept_two, kept_slope_two,
    blocks, params, features, filter_mid, table_high, table_low, back_high, back_low,
    kept_grad_streams, grad_shared, grad_last,
    spectra, filtered, long_out, own_spectra, hidden_one, slope_one, hidden_two, slope_two,
    grad_streams, sums, lag_sums, grad_spectra, semaphores,
):
    copies = start_copies(
        [
            (kept_filtered, filtered),
            (kept_spectra, spectra),
            (kept_own_spectra, own_spectra),
            (kept_long_out, long_out),
            (kept_two, hidden_two),
            (kept_slope_two, slope_two),
            (kept_one, hidden_one),
            (kept_slope_one, slope_one),
        ],
        semaphores,
    )
    count = blocks.shape[0]
    hidden = filter_mid.shape[0]
    wide = 3 * ROWS
    grad_gated = blocks[...].astype(f32)[:, ROWS : 2 * ROWS, :]
    wait_copies(copies[:4])
    query = filtered[:, :ROWS, :]
    grad_long = (grad_gated * query).reshape(count * ROWS, BLOCK).astype(bf16)
    spectrum = table_dot(grad_long, table_high[...], table_low[...])
    grad_spectra[...] = rows_of(spectrum, ROWS)
    sign = parity()
    after = None
    for block in reversed(range(count)):
        back_real = jnp.zeros((ROWS, BLOCK), f32)
        back_imag = jnp.zeros((ROWS, BLOCK), f32)
        lag_real = jnp.zeros((ROWS, BLOCK), f32)
        lag_imag = jnp.zeros((ROWS, BLOCK), f32)
        for target in range(block, count):
            grad_real = grad_spectra[target, :, :BLOCK]
            grad_imag = grad_spectra[target, :, BLOCK:]
            filter_real = spectra[target - block, :, :BLOCK]
            filter_imag = spectra[target - block, :, BLOCK:]
            back_real = back_real + filter_real * grad_real + filter_imag * grad_imag
            back_imag = back_imag + filter_real * grad_imag - filter_imag * grad_real
            own_real = own_spectra[target - block, :, :BLOCK]
            own_imag = own_spectra[target - block, :, BLOCK:]
            lag_real = lag_real + own_real * grad_real + own_imag * grad_imag
            lag_imag = lag_imag + own_real * grad_imag - own_imag * grad_real
        at = slice(block * ROWS, (block + 1) * ROWS)
        sums[at, :BLOCK] = back_real
        sums[at, BLOCK:] = back_imag
        if after is None:
            lag_sums[at, :BLOCK] = lag_real
            lag_sums[at, BLOCK:] = lag_imag
        else:
            lag_sums[at, :BLOCK] = lag_real + sign * after[1]
            lag_sums[at, BLOCK:] = lag_imag - sign * after[0]
        after = (lag_real, lag_imag)
    back = table_dot(sums[...], back_high[...], back_low[...])
    skip = params[:, SKIP : SKIP + 1][None]
    grad_product = rows_of(back, ROWS) + skip * rows_of(grad_long.astype(f32), ROWS)
    grads = [
        grad_gated * long_out[...],
        grad_product * filtered[:, 2 * ROWS :, :],
        grad_product * filtered[:, ROWS : 2 * ROWS, :],
    ]
    lane = lax.broadcasted_iota(jnp.int32, (count * ROWS, BLOCK), 1)
    tail = jnp.zeros((ROWS, BLOCK), f32)
    adjoint = []
    for stream in range(3):
        value = grads[stream].reshape(count * ROWS, BLOCK)
        total = params[:, stream * 3 : stream * 3 + 1][None] * grads[stream]
        for by in (1, 2):
            rolled = pltpu.roll(value, BLOCK - by, 1)
            following = jnp.concatenate([rolled[ROWS:], tail], axis=0)
            moved = jnp.where(lane >= BLOCK - by, following, rolled)
            column = stream * 3 + by
            total = total + params[:, column : column + 1][None] * rows_of(moved, ROWS)
        adjoint.append(total)
    half = BLOCK // 2
    packed = [part[:, :, :half] for part in adjoint] + [part[:, :, half:] for part in adjoint]
    grad_streams[...] = jnp.concatenate(packed, axis=1).astype(bf16)
    streams_copy = pltpu.make_async_copy(grad_streams, kept_grad_streams, semaphores.at[8])
    streams_copy.start()
    wait_copies(copies[4:])

    lags = table_dot(lag_sums[...], back_high[...], back_low[...])
    decay = params[:, DECAY : DECAY + 1]
    last = params[:, OUT : OUT + hidden]
    raw = [
        lags[block * ROWS : (block + 1) * ROWS] * envelope(decay, block)
        for block in range(count)
    ]
    total_last = jnp.zeros((ROWS, hidden), f32)
    total_mid = jnp.zeros((hidden, hidden), f32)
    total_in = jnp.zeros((features.shape[0], hidden), f32)
    across = ((1,), (1,))
    for block in range(count):
        at = slice(block * BLOCK, (block + 1) * BLOCK)
        total_last = total_last + close_dot(raw[block], hidden_two[:, at], across)
        grad_two = close_dot(last, raw[block], ((0,), (0,))) * slope_two[:, at]
        total_mid = total_mid + close_dot(hidden_one[:, at], grad_two, across)
        grad_one = close_dot(filter_mid[...], grad_two) * slope_one[:, at]
        total_in = total_in + close_dot(features[:, at], grad_one, across)
    grad_shared[...] = jnp.concatenate([total_in, total_mid], axis=0).astype(bf16)
    high, low = halves(total_last)
    grad_last[...] = jnp.concatenate([high.astype(f32), low.astype(f32)], axis=0).astype(bf16)
    streams_copy.wait()


def pack_kernel(far_weight, far_cotangent, packed, weight, cotangent, semaphores):
    wait_copies(
        start_copies([(far_weight, weight), (far_cotangent, cotangent)], semaphores)
    )
    side = packed.shape[0]
    channels, tokens = cotangent.shape
    for i in range(side):
        packed[i, :, :tokens] = cotangent[...]
        pieces = [
            weight[:, (a * side + i) * channels : (a * side + i + 1) * channels]
            for a in range(side)
        ]
        packed[i, :, tokens:] = jnp.concatenate(pieces, axis=1)


NEAR, FAR = pltpu.VMEM, pltpu.HBM


def call(kernel, outs, scratch, copies, *operands):
    semaphores = [pltpu.SemaphoreType.DMA((copies,))] if copies else []
    return pl.pallas_call(
        kernel,
        out_shape=[
            pltpu.HBM(shape, kind) if place is FAR else jax.ShapeDtypeStruct(shape, kind)
            for place, shape, kind in outs
        ],
        in_specs=[pl.BlockSpec(memory_space=place) for place, _ in operands],
        out_specs=[pl.BlockSpec(memory_space=place) for place, _, _ in outs],
        scratch_shapes=[pltpu.VMEM(shape, kind) for shape, kind in scratch] + semaphores,
        compiler_params=pltpu.CompilerParams(vmem_limit_bytes=VMEM_LIMIT),
    )(
        *[
            pltpu.with_memory_space_constraint(operand, FAR) if place is FAR else operand
            for place, operand in operands
        ]
    )


def exchange(value, axis, groups=None):
    return lax.all_to_all(value, axis, 0, 0, tiled=True, axis_index_groups=groups)


def shards(
    streams, short_taps, filter_in, filter_mid, filter_out, decay_rate, skip_gain, out_weight,
    grad_out,
):
    channels, tokens = streams.shape[1:]
    blocks = lax.axis_size("ctx")
    owners = lax.axis_size("ch")
    me = lax.axis_index("ctx")
    length = blocks * tokens
    share = channels // blocks
    hidden = filter_in.shape[1]
    band_rows = filter_in.shape[0]
    side = int(math.isqrt(owners))
    near_groups = [[a * side + i for i in range(side)] for a in range(side)]
    far_groups = [[a * side + i for a in range(side)] for i in range(side)]
    places = side // 2
    place_groups = [group[h * places : (h + 1) * places] for group in far_groups for h in range(2)]
    half = lax.axis_index("ch") // (places * side)
    chips = blocks // 2
    core = me % 2
    core_pairs = [(k, k ^ 1) for k in range(blocks)]
    chip_groups = [[2 * z + c for z in range(chips)] for c in range(2)]

    def in_order(here, there):
        second = core == 1
        return [jnp.where(second, there, here), jnp.where(second, here, there)]

    def between_cores(value, axis):
        here = lax.dynamic_index_in_dim(value, core, axis, False)
        there = lax.dynamic_index_in_dim(value, 1 - core, axis, False)
        return in_order(here, lax.ppermute(there, "ctx", core_pairs))
    group = side * channels
    pad_rows = ROWS - share
    tables = [jnp.asarray(t) for t in transform_tables()]
    features = jnp.asarray(position_features(band_rows // 2, length))

    (sent,) = call(
        pack_kernel,
        [(NEAR, (side, channels, tokens + group), bf16)],
        [(out_weight.shape, bf16), (grad_out.shape, bf16)],
        2,
        (FAR, out_weight), (FAR, grad_out),
    )
    sent = exchange(sent, "ch", near_groups)
    cotangent = sent[:, :, :tokens].reshape(group, tokens)
    weight = sent[:, :, tokens:].reshape(group, group)
    grad_terms = lax.dot_general(
        weight, cotangent, (((0,), (0,)), ((), ())), preferred_element_type=f32
    ).astype(bf16)
    grad_terms = between_cores(grad_terms.reshape(side, chips, 2, share, tokens), 2)
    grad_terms = jnp.stack(grad_terms, axis=1).reshape(2, places, channels, tokens)
    received = lax.ppermute(
        lax.dynamic_index_in_dim(grad_terms, 1 - half, 0, False),
        "ch",
        [(j, (j + places * side) % owners) for j in range(owners)],
    )
    grad_terms = lax.dynamic_index_in_dim(grad_terms, half, 0, False)
    grad_terms = (grad_terms.astype(f32) + received.astype(f32)).astype(bf16)
    grad_terms = exchange(grad_terms, "ch", place_groups)
    grad_gated = jnp.sum(grad_terms.astype(f32), axis=0).astype(bf16)

    params = jnp.concatenate(
        [
            short_taps.transpose(1, 0, 2).reshape(channels, 9),
            decay_rate[:, None],
            skip_gain[:, None],
            filter_out.T,
        ],
        axis=1,
    )
    params = lax.dynamic_slice_in_dim(params, me * share, share, 0)
    params = jnp.pad(params, ((0, pad_rows), (0, 128 - params.shape[1])))

    def near(*values):
        return [(NEAR, value) for value in values]

    def far_like(shapes):
        return [(FAR,) + shape for shape in shapes]

    wave = ((hidden, length), f32)
    spectrum = ((blocks, ROWS, 2 * tokens), f32)
    kept_waves = [wave] * 4 + [spectrum]
    *waves, spectra = call(
        network_kernel, far_like(kept_waves), kept_waves + [((blocks * ROWS, tokens), f32)], 5,
        *near(features, filter_in, filter_mid, params, tables[0], tables[1]),
    )

    by_share = streams.reshape(3, blocks, share, tokens).transpose(1, 0, 2, 3)
    by_share = jnp.pad(by_share, ((0, 0), (0, 0), (0, pad_rows), (0, 0)))
    by_share = between_cores(by_share.reshape(chips, 2, 3 * ROWS, tokens), 1)
    by_share = jnp.concatenate(by_share, axis=1)
    by_share, spectra = lax.optimization_barrier((by_share, spectra))
    sequence = exchange(by_share, "ctx", chip_groups).reshape(blocks, 3 * ROWS, tokens)
    kept = [
        ((blocks * ROWS, tokens), bf16),
        ((blocks, 3 * ROWS, tokens), f32),
        ((blocks, ROWS, tokens), f32),
        spectrum,
    ]
    gated, filtered, long_out, own_spectra = call(
        forward_kernel, far_like(kept), kept + [((blocks * ROWS, 2 * tokens), f32)], 4,
        *near(sequence, params, spectra, *tables),
    )

    turned = grad_gated.reshape(2, chips, share, tokens).transpose(1, 0, 2, 3)
    turned = jnp.pad(turned, ((0, 0), (0, 0), (0, pad_rows), (0, 0)))
    first, second = between_cores(gated.reshape(chips, 2, ROWS, tokens), 1)
    turned = jnp.concatenate([first, turned[:, 0], second, turned[:, 1]], axis=1)
    turned = exchange(turned, "ctx", chip_groups).reshape(blocks, 2 * ROWS, tokens)
    own_gated = turned[:, :share, :].reshape(channels, tokens)

    packed_streams = ((blocks, 6 * ROWS, tokens // 2), bf16)
    grad_packed, grad_shared, grad_last = call(
        backward_kernel,
        [
            (FAR,) + packed_streams,
            (NEAR, (band_rows + hidden, hidden), bf16),
            (NEAR, (2 * ROWS, hidden), bf16),
        ],
        [spectrum, kept[1], kept[2], spectrum]
        + [wave] * 4
        + [packed_streams]
        + [((blocks * ROWS, 2 * tokens), f32)] * 2
        + [spectrum],
        9,
        *[(FAR, value) for value in (spectra, filtered, long_out, own_spectra, *waves)],
        *near(turned, params, features, filter_mid, *tables),
    )

    shared_rows = grad_shared.size // tokens
    sent = jnp.concatenate([own_gated, grad_shared.reshape(shared_rows, tokens)], axis=0)
    sent = exchange(
        jnp.broadcast_to(sent[None], (side,) + sent.shape), "ch", far_groups
    )
    all_gated = sent[:, :channels].reshape(group, tokens)
    shared = jnp.sum(sent[:, channels:].astype(f32), axis=0)

    out_terms = jnp.dot(weight, all_gated, preferred_element_type=f32).astype(bf16)
    def both_halves(value):
        high = lax.reduce_precision(value, 8, 7)
        return high.astype(bf16), (value - high).astype(bf16)

    rows = side * share
    portion = (band_rows + hidden) // blocks
    by_core = cotangent.reshape(side, chips, 2, share, tokens).transpose(2, 1, 0, 3, 4)
    shared = shared.reshape(chips, 2, portion, hidden)
    grad_packed = grad_packed.reshape((chips, 2) + grad_packed.shape[1:])

    def parts_for(which):
        left = lax.dynamic_index_in_dim(by_core, which, 0, False).reshape(chips * rows, tokens)
        terms = lax.dot_general(
            left, all_gated, (((1,), (1,)), ((), ())), preferred_element_type=f32
        ).reshape(chips, rows, group)
        return (
            terms,
            lax.dynamic_index_in_dim(shared, which, 1, False),
            lax.dynamic_index_in_dim(grad_packed, which, 1, False),
        )

    def joined(terms, shared, lasts, packed):
        high, low = both_halves(shared)
        small = jnp.concatenate([high, low] + lasts, axis=1)
        small = jnp.pad(small, ((0, 0), (0, rows - small.shape[1]), (0, 0)))
        return jnp.concatenate([terms.astype(bf16), small] + packed, axis=2)

    last_here = jnp.broadcast_to(grad_last[None], (chips,) + grad_last.shape)
    terms, shared_part, packed = parts_for(1 - core)
    sent = joined(terms, shared_part, [last_here], [packed])
    sent = lax.ppermute(sent, "ctx", core_pairs)
    terms, shared_part, packed = parts_for(core)
    terms = terms + sent[:, :, :group].astype(f32)
    small = sent[:, :, group : group + hidden]
    shared_part = (
        shared_part
        + small[:, :portion].astype(f32)
        + small[:, portion : 2 * portion].astype(f32)
    )
    last_at = 2 * portion
    last_there = small[:, last_at : last_at + 2 * ROWS]
    packed_there = sent[:, :, group + hidden :]
    sent = joined(
        terms, shared_part, in_order(last_here, last_there), in_order(packed, packed_there)
    )
    sent = exchange(sent, "ctx", chip_groups)
    weight_share = jnp.sum(sent[:, :, :group].astype(f32), axis=0).astype(bf16)
    small = sent[:, :, group : group + hidden].astype(f32)
    shared = jnp.sum(small[:, :portion] + small[:, portion : 2 * portion], axis=0)
    lasts = small[:, last_at : last_at + 4 * ROWS].reshape(blocks, 2, ROWS, hidden)[:, :, :share]
    grad_filter_out = jnp.sum(lasts, axis=1).reshape(channels, hidden).T
    packed = sent[:, :, group + hidden :].reshape(chips, 2, 3, ROWS, 2, tokens // 2)
    grad_streams = (
        packed[:, :, :, :share].transpose(2, 0, 4, 3, 1, 5).reshape(3, channels, tokens)
    )

    high, low = both_halves(shared)
    width = 3 * tokens
    tail = jnp.concatenate([high, low], axis=0).reshape(2 * portion * hidden // tokens, tokens)
    weight_rows = jnp.pad(
        weight_share.reshape(side, share, group), ((0, 0), (0, 0), (0, width - group))
    ).reshape(side, share * 3, tokens)
    sent = jnp.concatenate(
        [
            out_terms.reshape(side, channels, tokens),
            weight_rows,
            jnp.broadcast_to(tail[None], (side,) + tail.shape),
        ],
        axis=1,
    )
    sent = exchange(sent, "ch", near_groups)
    layer_out = jnp.sum(sent[:, :channels].astype(f32), axis=0).astype(bf16)
    weight_rows = sent[:, channels : channels + 3 * share].reshape(side, share, width)[:, :, :group]
    weight_rows = weight_rows.reshape(side, share, side, channels).transpose(1, 2, 0, 3)
    weight_rows = weight_rows.reshape(share, owners * channels)
    tail = jnp.sum(sent[:, channels + 3 * share :].astype(f32), axis=0)
    tail = tail.reshape(2, portion * hidden)
    high, low = both_halves(tail[0] + tail[1])

    tail = jnp.concatenate([high, low])
    spare = -tail.size % (share * 128)
    tail = jnp.pad(tail, (0, spare)).reshape(share, -1)
    sent = lax.all_gather(jnp.concatenate([weight_rows, tail], axis=1), "ctx", axis=0)
    grad_out_weight = sent[:, :, : weight_rows.shape[1]].reshape(channels, -1).astype(f32)
    tail = sent[:, :, weight_rows.shape[1] :].reshape(blocks, -1).astype(f32)
    size = portion * hidden
    shared = (tail[:, :size] + tail[:, size : 2 * size]).reshape(band_rows + hidden, hidden)
    return (
        layer_out, grad_streams, shared[:band_rows], shared[band_rows:], grad_filter_out,
        grad_out_weight,
    )


def solution(mesh):
    return jax.shard_map(
        shards,
        mesh=mesh,
        in_specs=(
            P(None, "ch", "ctx"),
            P(None, "ch", None),
            P(),
            P(),
            P(None, "ch"),
            P("ch"),
            P("ch"),
            P("ch", None),
            P("ch", "ctx"),
        ),
        out_specs=(P("ch", "ctx"), P(None, "ch", "ctx"), P(), P(), P(None, "ch"), P("ch", None)),
        check_vma=False,
    )
```

```python
import functools
import math

import jax
import jax.numpy as jnp
import numpy as np
from jax import lax
from jax.experimental import pallas as pl
from jax.experimental.pallas import tpu as pltpu
from jax.sharding import PartitionSpec as P

f32 = jnp.float32
bf16 = jnp.bfloat16

BLOCK = 256
ROWS = 8
VMEM_LIMIT = 16 * 1024 * 1024


def split_table(table):
    high = table.astype(np.float32).astype(jnp.bfloat16)
    low = (table - high.astype(np.float64)).astype(np.float32).astype(jnp.bfloat16)
    return high, low


@functools.lru_cache(maxsize=None)
def transform_tables():
    frequency = np.arange(BLOCK)
    token = np.arange(BLOCK)
    angle = np.pi * ((2 * frequency[None, :] + 1) * token[:, None] % (4 * BLOCK)) / (2 * BLOCK)
    forward = np.concatenate([np.cos(angle), -np.sin(angle)], axis=1)
    return split_table(forward) + split_table(forward.T / BLOCK)


@functools.lru_cache(maxsize=None)
def position_features(band_count, length):
    wrapped = (np.arange(1, band_count + 1)[:, None] * np.arange(length)[None, :]) % length
    phases = 2.0 * np.pi / length * wrapped
    return np.concatenate([np.cos(phases), np.sin(phases)], axis=0).astype(np.float32)


def halves(value):
    high = value.astype(bf16)
    return high, (value - high.astype(f32)).astype(bf16)


def plain_dot(left, right, dims):
    return lax.dot_general(left, right, (dims, ((), ())), preferred_element_type=f32)


def close_dot(left, right, dims=((1,), (0,))):
    left_high, left_low = halves(left)
    right_high, right_low = halves(right)
    return (
        plain_dot(left_high, right_high, dims)
        + plain_dot(left_high, right_low, dims)
        + plain_dot(left_low, right_high, dims)
    )


def table_dot(left, high, low):
    dims = ((1,), (0,))
    if left.dtype == bf16:
        return plain_dot(left, high, dims) + plain_dot(left, low, dims)
    left_high, left_low = halves(left)
    return (
        plain_dot(left_high, high, dims)
        + plain_dot(left_high, low, dims)
        + plain_dot(left_low, high, dims)
    )


def sine_and_cosine(value):
    turns = jnp.floor(value * (2.0 / math.pi) + 0.5)
    rest = value - turns * 1.5703125
    rest = rest - turns * 4.837512969970703125e-4
    rest = rest - turns * 7.54978994876864e-8
    square = rest * rest
    sine = rest + rest * square * (
        -1.6666654611e-1 + square * (8.3321608736e-3 + square * -1.9515295891e-4)
    )
    cosine = (
        1.0
        - 0.5 * square
        + square
        * square
        * (4.166664568298827e-2 + square * (-1.388731625493765e-3 + square * 2.443315711809948e-5))
    )
    quadrant = turns.astype(jnp.int32)
    odd = (quadrant & 1) == 1
    sine_out = jnp.where(odd, cosine, sine)
    cosine_out = jnp.where(odd, sine, cosine)
    sine_out = jnp.where((quadrant & 2) == 2, -sine_out, sine_out)
    cosine_out = jnp.where(((quadrant + 1) & 2) == 2, -cosine_out, cosine_out)
    return sine_out, cosine_out


def envelope(decay, block):
    lag = (lax.broadcasted_iota(jnp.int32, (ROWS, BLOCK), 1) + block * BLOCK).astype(f32)
    return jnp.exp(-decay * lag) * jnp.sqrt(decay)


def parity():
    odd = lax.broadcasted_iota(jnp.int32, (ROWS, BLOCK), 1) & 1
    return (1 - 2 * odd).astype(f32)


DECAY, SKIP, OUT = 9, 10, 11


def start_copies(pairs, semaphores):
    copies = [
        pltpu.make_async_copy(source, target, semaphores.at[i])
        for i, (source, target) in enumerate(pairs)
    ]
    for copy in copies:
        copy.start()
    return copies


def wait_copies(copies):
    for copy in copies:
        copy.wait()


def network_kernel(
    features, filter_in, filter_mid, params, table_high, table_low,
    kept_one, kept_slope_one, kept_two, kept_slope_two, kept_spectra,
    hidden_one, slope_one, hidden_two, slope_two, spectra, taps_scratch, semaphores,
):
    count = features.shape[1] // BLOCK
    hidden = filter_in.shape[1]
    decay = params[:, DECAY : DECAY + 1]
    last = params[:, OUT : OUT + hidden]
    for block in range(count):
        at = slice(block * BLOCK, (block + 1) * BLOCK)
        sine, cosine = sine_and_cosine(
            close_dot(filter_in[...], features[:, at], ((0,), (0,)))
        )
        hidden_one[:, at] = sine
        slope_one[:, at] = cosine
        sine, cosine = sine_and_cosine(close_dot(filter_mid[...], sine, ((0,), (0,))))
        hidden_two[:, at] = sine
        slope_two[:, at] = cosine
        raw = close_dot(last, sine)
        taps_scratch[block * ROWS : (block + 1) * ROWS, :] = raw * envelope(decay, block)
    copies = start_copies(
        [
            (hidden_one, kept_one),
            (slope_one, kept_slope_one),
            (hidden_two, kept_two),
            (slope_two, kept_slope_two),
        ],
        semaphores,
    )
    spectrum = table_dot(taps_scratch[...], table_high[...], table_low[...])
    sign = parity()
    for block in range(count):
        real = spectrum[block * ROWS : (block + 1) * ROWS, :BLOCK]
        imag = spectrum[block * ROWS : (block + 1) * ROWS, BLOCK:]
        if block:
            before = slice((block - 1) * ROWS, block * ROWS)
            real = real - sign * spectrum[before, BLOCK:]
            imag = imag + sign * spectrum[before, :BLOCK]
        spectra[block, :, :BLOCK] = real
        spectra[block, :, BLOCK:] = imag
    last_copy = pltpu.make_async_copy(spectra, kept_spectra, semaphores.at[4])
    last_copy.start()
    wait_copies(copies + [last_copy])


def rows_of(value, rows):
    return value.reshape(value.shape[0] // rows, rows, value.shape[1])


def forward_kernel(
    blocks, params, spectra, table_high, table_low, back_high, back_low,
    kept_gated, kept_filtered, kept_long_out, kept_spectra,
    gated, filtered, long_out, own_spectra, sums, semaphores,
):
    count = blocks.shape[0]
    wide = 3 * ROWS
    raw = blocks[...].astype(f32).reshape(count * wide, BLOCK)
    lane = lax.broadcasted_iota(jnp.int32, (count * wide, BLOCK), 1)
    lead = jnp.zeros((wide, BLOCK), f32)
    shifted = [raw]
    for by in (1, 2):
        rolled = pltpu.roll(raw, by, 1)
        before = jnp.concatenate([lead, rolled[:-wide]], axis=0)
        shifted.append(jnp.where(lane < by, before, rolled))
    shifted = [rows_of(value, wide) for value in shifted]
    streams = []
    for stream in range(3):
        at = slice(stream * ROWS, (stream + 1) * ROWS)
        total = None
        for tap in range(3):
            column = stream * 3 + tap
            term = params[:, column : column + 1][None] * shifted[tap][:, at, :]
            total = term if total is None else total + term
        filtered[:, at, :] = total
        streams.append(total)
    product = (streams[1] * streams[2]).astype(bf16).astype(f32).reshape(count * ROWS, BLOCK)
    spectrum = table_dot(product.astype(bf16), table_high[...], table_low[...])
    own_spectra[...] = rows_of(spectrum, ROWS)
    for block in range(count):
        real = jnp.zeros((ROWS, BLOCK), f32)
        imag = jnp.zeros((ROWS, BLOCK), f32)
        for source in range(block + 1):
            filter_real = spectra[block - source, :, :BLOCK]
            filter_imag = spectra[block - source, :, BLOCK:]
            own_real = own_spectra[source, :, :BLOCK]
            own_imag = own_spectra[source, :, BLOCK:]
            real = real + filter_real * own_real - filter_imag * own_imag
            imag = imag + filter_real * own_imag + filter_imag * own_real
        sums[block * ROWS : (block + 1) * ROWS, :BLOCK] = real
        sums[block * ROWS : (block + 1) * ROWS, BLOCK:] = imag
    conv = table_dot(sums[...], back_high[...], back_low[...])
    skip = params[:, SKIP : SKIP + 1][None]
    result = rows_of(conv, ROWS) + skip * rows_of(product, ROWS)
    long_out[...] = result
    gated[...] = (streams[0] * result).reshape(count * ROWS, BLOCK).astype(bf16)
    wait_copies(
        start_copies(
            [
                (gated, kept_gated),
                (filtered, kept_filtered),
                (long_out, kept_long_out),
                (own_spectra, kept_spectra),
            ],
            semaphores,
        )
    )


def backward_kernel(
    kept_spectra, kept_filtered, kept_long_out, kept_own_spectra,
    kept_one, kept_slope_one, kept_two, kept_slope_two,
    blocks, params, features, filter_mid, table_high, table_low, back_high, back_low,
    kept_grad_streams, grad_shared, grad_last,
    spectra, filtered, long_out, own_spectra, hidden_one, slope_one, hidden_two, slope_two,
    grad_streams, sums, lag_sums, grad_spectra, semaphores,
):
    copies = start_copies(
        [
            (kept_filtered, filtered),
            (kept_spectra, spectra),
            (kept_own_spectra, own_spectra),
            (kept_long_out, long_out),
            (kept_two, hidden_two),
            (kept_slope_two, slope_two),
            (kept_one, hidden_one),
            (kept_slope_one, slope_one),
        ],
        semaphores,
    )
    count = blocks.shape[0]
    hidden = filter_mid.shape[0]
    wide = 3 * ROWS
    grad_gated = blocks[...].astype(f32)[:, ROWS : 2 * ROWS, :]
    wait_copies(copies[:4])
    query = filtered[:, :ROWS, :]
    grad_long = (grad_gated * query).reshape(count * ROWS, BLOCK).astype(bf16)
    spectrum = table_dot(grad_long, table_high[...], table_low[...])
    grad_spectra[...] = rows_of(spectrum, ROWS)
    sign = parity()
    after = None
    for block in reversed(range(count)):
        back_real = jnp.zeros((ROWS, BLOCK), f32)
        back_imag = jnp.zeros((ROWS, BLOCK), f32)
        lag_real = jnp.zeros((ROWS, BLOCK), f32)
        lag_imag = jnp.zeros((ROWS, BLOCK), f32)
        for target in range(block, count):
            grad_real = grad_spectra[target, :, :BLOCK]
            grad_imag = grad_spectra[target, :, BLOCK:]
            filter_real = spectra[target - block, :, :BLOCK]
            filter_imag = spectra[target - block, :, BLOCK:]
            back_real = back_real + filter_real * grad_real + filter_imag * grad_imag
            back_imag = back_imag + filter_real * grad_imag - filter_imag * grad_real
            own_real = own_spectra[target - block, :, :BLOCK]
            own_imag = own_spectra[target - block, :, BLOCK:]
            lag_real = lag_real + own_real * grad_real + own_imag * grad_imag
            lag_imag = lag_imag + own_real * grad_imag - own_imag * grad_real
        at = slice(block * ROWS, (block + 1) * ROWS)
        sums[at, :BLOCK] = back_real
        sums[at, BLOCK:] = back_imag
        if after is None:
            lag_sums[at, :BLOCK] = lag_real
            lag_sums[at, BLOCK:] = lag_imag
        else:
            lag_sums[at, :BLOCK] = lag_real + sign * after[1]
            lag_sums[at, BLOCK:] = lag_imag - sign * after[0]
        after = (lag_real, lag_imag)
    back = table_dot(sums[...], back_high[...], back_low[...])
    skip = params[:, SKIP : SKIP + 1][None]
    grad_product = rows_of(back, ROWS) + skip * rows_of(grad_long.astype(f32), ROWS)
    grads = [
        grad_gated * long_out[...],
        grad_product * filtered[:, 2 * ROWS :, :],
        grad_product * filtered[:, ROWS : 2 * ROWS, :],
    ]
    lane = lax.broadcasted_iota(jnp.int32, (count * ROWS, BLOCK), 1)
    tail = jnp.zeros((ROWS, BLOCK), f32)
    adjoint = []
    for stream in range(3):
        value = grads[stream].reshape(count * ROWS, BLOCK)
        total = params[:, stream * 3 : stream * 3 + 1][None] * grads[stream]
        for by in (1, 2):
            rolled = pltpu.roll(value, BLOCK - by, 1)
            following = jnp.concatenate([rolled[ROWS:], tail], axis=0)
            moved = jnp.where(lane >= BLOCK - by, following, rolled)
            column = stream * 3 + by
            total = total + params[:, column : column + 1][None] * rows_of(moved, ROWS)
        adjoint.append(total)
    half = BLOCK // 2
    packed = [part[:, :, :half] for part in adjoint] + [part[:, :, half:] for part in adjoint]
    grad_streams[...] = jnp.concatenate(packed, axis=1).astype(bf16)
    streams_copy = pltpu.make_async_copy(grad_streams, kept_grad_streams, semaphores.at[8])
    streams_copy.start()
    wait_copies(copies[4:])

    lags = table_dot(lag_sums[...], back_high[...], back_low[...])
    decay = params[:, DECAY : DECAY + 1]
    last = params[:, OUT : OUT + hidden]
    raw = [
        lags[block * ROWS : (block + 1) * ROWS] * envelope(decay, block)
        for block in range(count)
    ]
    total_last = jnp.zeros((ROWS, hidden), f32)
    total_mid = jnp.zeros((hidden, hidden), f32)
    total_in = jnp.zeros((features.shape[0], hidden), f32)
    across = ((1,), (1,))
    for block in range(count):
        at = slice(block * BLOCK, (block + 1) * BLOCK)
        total_last = total_last + close_dot(raw[block], hidden_two[:, at], across)
        grad_two = close_dot(last, raw[block], ((0,), (0,))) * slope_two[:, at]
        total_mid = total_mid + close_dot(hidden_one[:, at], grad_two, across)
        grad_one = close_dot(filter_mid[...], grad_two) * slope_one[:, at]
        total_in = total_in + close_dot(features[:, at], grad_one, across)
    grad_shared[...] = jnp.concatenate([total_in, total_mid], axis=0).astype(bf16)
    high, low = halves(total_last)
    grad_last[...] = jnp.concatenate([high.astype(f32), low.astype(f32)], axis=0).astype(bf16)
    streams_copy.wait()


def pack_kernel(far_weight, far_cotangent, packed, weight, cotangent, semaphores):
    wait_copies(
        start_copies([(far_weight, weight), (far_cotangent, cotangent)], semaphores)
    )
    side = packed.shape[0]
    channels, tokens = cotangent.shape
    for i in range(side):
        packed[i, :, :tokens] = cotangent[...]
        pieces = [
            weight[:, (a * side + i) * channels : (a * side + i + 1) * channels]
            for a in range(side)
        ]
        packed[i, :, tokens:] = jnp.concatenate(pieces, axis=1)


NEAR, FAR = pltpu.VMEM, pltpu.HBM


def call(kernel, outs, scratch, copies, *operands):
    semaphores = [pltpu.SemaphoreType.DMA((copies,))] if copies else []
    return pl.pallas_call(
        kernel,
        out_shape=[
            pltpu.HBM(shape, kind) if place is FAR else jax.ShapeDtypeStruct(shape, kind)
            for place, shape, kind in outs
        ],
        in_specs=[pl.BlockSpec(memory_space=place) for place, _ in operands],
        out_specs=[pl.BlockSpec(memory_space=place) for place, _, _ in outs],
        scratch_shapes=[pltpu.VMEM(shape, kind) for shape, kind in scratch] + semaphores,
        compiler_params=pltpu.CompilerParams(vmem_limit_bytes=VMEM_LIMIT),
    )(
        *[
            pltpu.with_memory_space_constraint(operand, FAR) if place is FAR else operand
            for place, operand in operands
        ]
    )


def exchange(value, axis, groups=None):
    return lax.all_to_all(value, axis, 0, 0, tiled=True, axis_index_groups=groups)


def shards(
    streams, short_taps, filter_in, filter_mid, filter_out, decay_rate, skip_gain, out_weight,
    grad_out,
):
    channels, tokens = streams.shape[1:]
    blocks = lax.axis_size("ctx")
    owners = lax.axis_size("ch")
    me = lax.axis_index("ctx")
    length = blocks * tokens
    share = channels // blocks
    hidden = filter_in.shape[1]
    band_rows = filter_in.shape[0]
    side = int(math.isqrt(owners))
    near_groups = [[a * side + i for i in range(side)] for a in range(side)]
    far_groups = [[a * side + i for a in range(side)] for i in range(side)]
    places = side // 2
    place_groups = [group[h * places : (h + 1) * places] for group in far_groups for h in range(2)]
    half = lax.axis_index("ch") // (places * side)

    def other_half(value):
        pairs = [(j, (j + places * side) % owners) for j in range(owners)]
        return lax.ppermute(value, "ch", pairs)

    chips = blocks // 2
    core = me % 2
    core_pairs = [(k, k ^ 1) for k in range(blocks)]
    chip_groups = [[2 * z + c for z in range(chips)] for c in range(2)]

    def in_order(here, there):
        second = core == 1
        return [jnp.where(second, there, here), jnp.where(second, here, there)]

    def between_cores(value, axis):
        here = lax.dynamic_index_in_dim(value, core, axis, False)
        there = lax.dynamic_index_in_dim(value, 1 - core, axis, False)
        return in_order(here, lax.ppermute(there, "ctx", core_pairs))
    group = side * channels
    pad_rows = ROWS - share
    tables = [jnp.asarray(t) for t in transform_tables()]
    features = jnp.asarray(position_features(band_rows // 2, length))

    (sent,) = call(
        pack_kernel,
        [(NEAR, (side, channels, tokens + group), bf16)],
        [(out_weight.shape, bf16), (grad_out.shape, bf16)],
        2,
        (FAR, out_weight), (FAR, grad_out),
    )
    sent = exchange(sent, "ch", near_groups)
    cotangent = sent[:, :, :tokens].reshape(group, tokens)
    weight = sent[:, :, tokens:].reshape(group, group)
    grad_terms = lax.dot_general(
        weight, cotangent, (((0,), (0,)), ((), ())), preferred_element_type=f32
    ).astype(bf16)
    grad_terms = between_cores(grad_terms.reshape(side, chips, 2, share, tokens), 2)
    grad_terms = jnp.stack(grad_terms, axis=1).reshape(2, places, channels, tokens)
    grad_terms = exchange(grad_terms.transpose(1, 0, 2, 3), "ch", place_groups)
    grad_terms = jnp.sum(grad_terms.astype(f32), axis=0)
    received = other_half(lax.dynamic_index_in_dim(grad_terms, 1 - half, 0, False).astype(bf16))
    grad_gated = lax.dynamic_index_in_dim(grad_terms, half, 0, False)
    grad_gated = (grad_gated + received.astype(f32)).astype(bf16)

    params = jnp.concatenate(
        [
            short_taps.transpose(1, 0, 2).reshape(channels, 9),
            decay_rate[:, None],
            skip_gain[:, None],
            filter_out.T,
        ],
        axis=1,
    )
    params = lax.dynamic_slice_in_dim(params, me * share, share, 0)
    params = jnp.pad(params, ((0, pad_rows), (0, 128 - params.shape[1])))

    def near(*values):
        return [(NEAR, value) for value in values]

    def far_like(shapes):
        return [(FAR,) + shape for shape in shapes]

    wave = ((hidden, length), f32)
    spectrum = ((blocks, ROWS, 2 * tokens), f32)
    kept_waves = [wave] * 4 + [spectrum]
    *waves, spectra = call(
        network_kernel, far_like(kept_waves), kept_waves + [((blocks * ROWS, tokens), f32)], 5,
        *near(features, filter_in, filter_mid, params, tables[0], tables[1]),
    )

    by_share = streams.reshape(3, blocks, share, tokens).transpose(1, 0, 2, 3)
    by_share = jnp.pad(by_share, ((0, 0), (0, 0), (0, pad_rows), (0, 0)))
    by_share = between_cores(by_share.reshape(chips, 2, 3 * ROWS, tokens), 1)
    by_share = jnp.concatenate(by_share, axis=1)
    by_share, spectra = lax.optimization_barrier((by_share, spectra))
    sequence = exchange(by_share, "ctx", chip_groups).reshape(blocks, 3 * ROWS, tokens)
    kept = [
        ((blocks * ROWS, tokens), bf16),
        ((blocks, 3 * ROWS, tokens), f32),
        ((blocks, ROWS, tokens), f32),
        spectrum,
    ]
    gated, filtered, long_out, own_spectra = call(
        forward_kernel, far_like(kept), kept + [((blocks * ROWS, 2 * tokens), f32)], 4,
        *near(sequence, params, spectra, *tables),
    )

    turned = grad_gated.reshape(2, chips, share, tokens).transpose(1, 0, 2, 3)
    turned = jnp.pad(turned, ((0, 0), (0, 0), (0, pad_rows), (0, 0)))
    first, second = between_cores(gated.reshape(chips, 2, ROWS, tokens), 1)
    turned = jnp.concatenate([first, turned[:, 0], second, turned[:, 1]], axis=1)
    turned = exchange(turned, "ctx", chip_groups).reshape(blocks, 2 * ROWS, tokens)
    own_gated = turned[:, :share, :].reshape(channels, tokens)

    packed_streams = ((blocks, 6 * ROWS, tokens // 2), bf16)
    grad_packed, grad_shared, grad_last = call(
        backward_kernel,
        [
            (FAR,) + packed_streams,
            (NEAR, (band_rows + hidden, hidden), bf16),
            (NEAR, (2 * ROWS, hidden), bf16),
        ],
        [spectrum, kept[1], kept[2], spectrum]
        + [wave] * 4
        + [packed_streams]
        + [((blocks * ROWS, 2 * tokens), f32)] * 2
        + [spectrum],
        9,
        *[(FAR, value) for value in (spectra, filtered, long_out, own_spectra, *waves)],
        *near(turned, params, features, filter_mid, *tables),
    )

    shared_rows = grad_shared.size // tokens
    sent = jnp.concatenate([own_gated, grad_shared.reshape(shared_rows, tokens)], axis=0)
    sent = exchange(
        jnp.broadcast_to(sent[None], (side,) + sent.shape), "ch", far_groups
    )
    all_gated = sent[:, :channels].reshape(group, tokens)
    shared = jnp.sum(sent[:, channels:].astype(f32), axis=0)

    out_terms = jnp.dot(weight, all_gated, preferred_element_type=f32).astype(bf16)
    def both_halves(value):
        high = lax.reduce_precision(value, 8, 7)
        return high.astype(bf16), (value - high).astype(bf16)

    rows = side * share
    portion = (band_rows + hidden) // blocks
    by_core = cotangent.reshape(side, chips, 2, share, tokens).transpose(2, 1, 0, 3, 4)
    shared = shared.reshape(chips, 2, portion, hidden)
    grad_packed = grad_packed.reshape((chips, 2) + grad_packed.shape[1:])

    def parts_for(which):
        left = lax.dynamic_index_in_dim(by_core, which, 0, False).reshape(chips * rows, tokens)
        terms = lax.dot_general(
            left, all_gated, (((1,), (1,)), ((), ())), preferred_element_type=f32
        ).reshape(chips, rows, group)
        return (
            terms,
            lax.dynamic_index_in_dim(shared, which, 1, False),
            lax.dynamic_index_in_dim(grad_packed, which, 1, False),
        )

    def joined(terms, shared, lasts, packed):
        high, low = both_halves(shared)
        small = jnp.concatenate([high, low] + lasts, axis=1)
        small = jnp.pad(small, ((0, 0), (0, rows - small.shape[1]), (0, 0)))
        return jnp.concatenate([terms.astype(bf16), small] + packed, axis=2)

    last_here = jnp.broadcast_to(grad_last[None], (chips,) + grad_last.shape)
    terms, shared_part, packed = parts_for(1 - core)
    sent = joined(terms, shared_part, [last_here], [packed])
    sent = lax.ppermute(sent, "ctx", core_pairs)
    terms, shared_part, packed = parts_for(core)
    terms = terms + sent[:, :, :group].astype(f32)
    small = sent[:, :, group : group + hidden]
    shared_part = (
        shared_part
        + small[:, :portion].astype(f32)
        + small[:, portion : 2 * portion].astype(f32)
    )
    last_at = 2 * portion
    last_there = small[:, last_at : last_at + 2 * ROWS]
    packed_there = sent[:, :, group + hidden :]
    sent = joined(
        terms, shared_part, in_order(last_here, last_there), in_order(packed, packed_there)
    )
    sent = exchange(sent, "ctx", chip_groups)
    weight_share = jnp.sum(sent[:, :, :group].astype(f32), axis=0).astype(bf16)
    small = sent[:, :, group : group + hidden].astype(f32)
    shared = jnp.sum(small[:, :portion] + small[:, portion : 2 * portion], axis=0)
    lasts = small[:, last_at : last_at + 4 * ROWS].reshape(blocks, 2, ROWS, hidden)[:, :, :share]
    grad_filter_out = jnp.sum(lasts, axis=1).reshape(channels, hidden).T
    packed = sent[:, :, group + hidden :].reshape(chips, 2, 3, ROWS, 2, tokens // 2)
    grad_streams = (
        packed[:, :, :, :share].transpose(2, 0, 4, 3, 1, 5).reshape(3, channels, tokens)
    )

    high, low = both_halves(shared)
    width = 3 * tokens
    tail = jnp.concatenate([high, low], axis=0).reshape(2 * portion * hidden // tokens, tokens)
    weight_rows = jnp.pad(
        weight_share.reshape(side, share, group), ((0, 0), (0, 0), (0, width - group))
    ).reshape(side, share * 3, tokens)
    sent = jnp.concatenate(
        [
            out_terms.reshape(side, channels, tokens),
            weight_rows,
            jnp.broadcast_to(tail[None], (side,) + tail.shape),
        ],
        axis=1,
    )
    sent = exchange(sent, "ch", near_groups)
    layer_out = jnp.sum(sent[:, :channels].astype(f32), axis=0).astype(bf16)
    weight_rows = sent[:, channels : channels + 3 * share].reshape(side, share, width)[:, :, :group]
    weight_rows = weight_rows.reshape(side, share, side, channels).transpose(1, 2, 0, 3)
    weight_rows = weight_rows.reshape(share, owners * channels)
    tail = jnp.sum(sent[:, channels + 3 * share :].astype(f32), axis=0)
    tail = tail.reshape(2, portion * hidden)
    high, low = both_halves(tail[0] + tail[1])

    tail = jnp.concatenate([high, low])
    spare = -tail.size % (share * 128)
    tail = jnp.pad(tail, (0, spare)).reshape(share, -1)
    sent = lax.all_gather(jnp.concatenate([weight_rows, tail], axis=1), "ctx", axis=0)
    grad_out_weight = sent[:, :, : weight_rows.shape[1]].reshape(channels, -1).astype(f32)
    tail = sent[:, :, weight_rows.shape[1] :].reshape(blocks, -1).astype(f32)
    size = portion * hidden
    shared = (tail[:, :size] + tail[:, size : 2 * size]).reshape(band_rows + hidden, hidden)
    return (
        layer_out, grad_streams, shared[:band_rows], shared[band_rows:], grad_filter_out,
        grad_out_weight,
    )


def solution(mesh):
    return jax.shard_map(
        shards,
        mesh=mesh,
        in_specs=(
            P(None, "ch", "ctx"),
            P(None, "ch", None),
            P(),
            P(),
            P(None, "ch"),
            P("ch"),
            P("ch"),
            P("ch", None),
            P("ch", "ctx"),
        ),
        out_specs=(P("ch", "ctx"), P(None, "ch", "ctx"), P(), P(), P(None, "ch"), P("ch", None)),
        check_vma=False,
    )
```

```python
import functools
import math

import jax
import jax.numpy as jnp
import numpy as np
from jax import lax
from jax.experimental import pallas as pl
from jax.experimental.pallas import tpu as pltpu
from jax.sharding import PartitionSpec as P

f32 = jnp.float32
bf16 = jnp.bfloat16

BLOCK = 256
ROWS = 8
VMEM_LIMIT = 16 * 1024 * 1024


def split_table(table):
    high = table.astype(np.float32).astype(jnp.bfloat16)
    low = (table - high.astype(np.float64)).astype(np.float32).astype(jnp.bfloat16)
    return high, low


@functools.lru_cache(maxsize=None)
def transform_tables():
    frequency = np.arange(BLOCK)
    token = np.arange(BLOCK)
    angle = np.pi * ((2 * frequency[None, :] + 1) * token[:, None] % (4 * BLOCK)) / (2 * BLOCK)
    forward = np.concatenate([np.cos(angle), -np.sin(angle)], axis=1)
    return split_table(forward) + split_table(forward.T / BLOCK)


@functools.lru_cache(maxsize=None)
def position_features(band_count, length):
    wrapped = (np.arange(1, band_count + 1)[:, None] * np.arange(length)[None, :]) % length
    phases = 2.0 * np.pi / length * wrapped
    return np.concatenate([np.cos(phases), np.sin(phases)], axis=0).astype(np.float32)


def halves(value):
    high = value.astype(bf16)
    return high, (value - high.astype(f32)).astype(bf16)


def plain_dot(left, right, dims):
    return lax.dot_general(left, right, (dims, ((), ())), preferred_element_type=f32)


def close_dot(left, right, dims=((1,), (0,))):
    left_high, left_low = halves(left)
    right_high, right_low = halves(right)
    return (
        plain_dot(left_high, right_high, dims)
        + plain_dot(left_high, right_low, dims)
        + plain_dot(left_low, right_high, dims)
    )


def table_dot(left, high, low):
    dims = ((1,), (0,))
    if left.dtype == bf16:
        return plain_dot(left, high, dims) + plain_dot(left, low, dims)
    left_high, left_low = halves(left)
    return (
        plain_dot(left_high, high, dims)
        + plain_dot(left_high, low, dims)
        + plain_dot(left_low, high, dims)
    )


def sine_and_cosine(value):
    turns = jnp.floor(value * (2.0 / math.pi) + 0.5)
    rest = value - turns * 1.5703125
    rest = rest - turns * 4.837512969970703125e-4
    rest = rest - turns * 7.54978994876864e-8
    square = rest * rest
    sine = rest + rest * square * (
        -1.6666654611e-1 + square * (8.3321608736e-3 + square * -1.9515295891e-4)
    )
    cosine = (
        1.0
        - 0.5 * square
        + square
        * square
        * (4.166664568298827e-2 + square * (-1.388731625493765e-3 + square * 2.443315711809948e-5))
    )
    quadrant = turns.astype(jnp.int32)
    odd = (quadrant & 1) == 1
    sine_out = jnp.where(odd, cosine, sine)
    cosine_out = jnp.where(odd, sine, cosine)
    sine_out = jnp.where((quadrant & 2) == 2, -sine_out, sine_out)
    cosine_out = jnp.where(((quadrant + 1) & 2) == 2, -cosine_out, cosine_out)
    return sine_out, cosine_out


def envelope(decay, block):
    lag = (lax.broadcasted_iota(jnp.int32, (ROWS, BLOCK), 1) + block * BLOCK).astype(f32)
    return jnp.exp(-decay * lag) * jnp.sqrt(decay)


def parity():
    odd = lax.broadcasted_iota(jnp.int32, (ROWS, BLOCK), 1) & 1
    return (1 - 2 * odd).astype(f32)


DECAY, SKIP, OUT = 9, 10, 11


def start_copies(pairs, semaphores):
    copies = [
        pltpu.make_async_copy(source, target, semaphores.at[i])
        for i, (source, target) in enumerate(pairs)
    ]
    for copy in copies:
        copy.start()
    return copies


def wait_copies(copies):
    for copy in copies:
        copy.wait()


def network_kernel(
    features, filter_in, filter_mid, params, table_high, table_low,
    kept_one, kept_slope_one, kept_two, kept_slope_two, kept_spectra,
    hidden_one, slope_one, hidden_two, slope_two, spectra, taps_scratch, semaphores,
):
    count = features.shape[1] // BLOCK
    hidden = filter_in.shape[1]
    decay = params[:, DECAY : DECAY + 1]
    last = params[:, OUT : OUT + hidden]
    for block in range(count):
        at = slice(block * BLOCK, (block + 1) * BLOCK)
        sine, cosine = sine_and_cosine(
            close_dot(filter_in[...], features[:, at], ((0,), (0,)))
        )
        hidden_one[:, at] = sine
        slope_one[:, at] = cosine
        sine, cosine = sine_and_cosine(close_dot(filter_mid[...], sine, ((0,), (0,))))
        hidden_two[:, at] = sine
        slope_two[:, at] = cosine
        raw = close_dot(last, sine)
        taps_scratch[block * ROWS : (block + 1) * ROWS, :] = raw * envelope(decay, block)
    copies = start_copies(
        [
            (hidden_one, kept_one),
            (slope_one, kept_slope_one),
            (hidden_two, kept_two),
            (slope_two, kept_slope_two),
        ],
        semaphores,
    )
    spectrum = table_dot(taps_scratch[...], table_high[...], table_low[...])
    sign = parity()
    for block in range(count):
        real = spectrum[block * ROWS : (block + 1) * ROWS, :BLOCK]
        imag = spectrum[block * ROWS : (block + 1) * ROWS, BLOCK:]
        if block:
            before = slice((block - 1) * ROWS, block * ROWS)
            real = real - sign * spectrum[before, BLOCK:]
            imag = imag + sign * spectrum[before, :BLOCK]
        spectra[block, :, :BLOCK] = real
        spectra[block, :, BLOCK:] = imag
    last_copy = pltpu.make_async_copy(spectra, kept_spectra, semaphores.at[4])
    last_copy.start()
    wait_copies(copies + [last_copy])


def rows_of(value, rows):
    return value.reshape(value.shape[0] // rows, rows, value.shape[1])


def forward_kernel(
    blocks, params, spectra, table_high, table_low, back_high, back_low,
    kept_gated, kept_filtered, kept_long_out, kept_spectra,
    gated, filtered, long_out, own_spectra, sums, semaphores,
):
    count = blocks.shape[0]
    wide = 3 * ROWS
    raw = blocks[...].astype(f32).reshape(count * wide, BLOCK)
    lane = lax.broadcasted_iota(jnp.int32, (count * wide, BLOCK), 1)
    lead = jnp.zeros((wide, BLOCK), f32)
    shifted = [raw]
    for by in (1, 2):
        rolled = pltpu.roll(raw, by, 1)
        before = jnp.concatenate([lead, rolled[:-wide]], axis=0)
        shifted.append(jnp.where(lane < by, before, rolled))
    shifted = [rows_of(value, wide) for value in shifted]
    streams = []
    for stream in range(3):
        at = slice(stream * ROWS, (stream + 1) * ROWS)
        total = None
        for tap in range(3):
            column = stream * 3 + tap
            term = params[:, column : column + 1][None] * shifted[tap][:, at, :]
            total = term if total is None else total + term
        filtered[:, at, :] = total
        streams.append(total)
    product = (streams[1] * streams[2]).astype(bf16).astype(f32).reshape(count * ROWS, BLOCK)
    spectrum = table_dot(product.astype(bf16), table_high[...], table_low[...])
    own_spectra[...] = rows_of(spectrum, ROWS)
    for block in range(count):
        real = jnp.zeros((ROWS, BLOCK), f32)
        imag = jnp.zeros((ROWS, BLOCK), f32)
        for source in range(block + 1):
            filter_real = spectra[block - source, :, :BLOCK]
            filter_imag = spectra[block - source, :, BLOCK:]
            own_real = own_spectra[source, :, :BLOCK]
            own_imag = own_spectra[source, :, BLOCK:]
            real = real + filter_real * own_real - filter_imag * own_imag
            imag = imag + filter_real * own_imag + filter_imag * own_real
        sums[block * ROWS : (block + 1) * ROWS, :BLOCK] = real
        sums[block * ROWS : (block + 1) * ROWS, BLOCK:] = imag
    conv = table_dot(sums[...], back_high[...], back_low[...])
    skip = params[:, SKIP : SKIP + 1][None]
    result = rows_of(conv, ROWS) + skip * rows_of(product, ROWS)
    long_out[...] = result
    gated[...] = (streams[0] * result).reshape(count * ROWS, BLOCK).astype(bf16)
    wait_copies(
        start_copies(
            [
                (gated, kept_gated),
                (filtered, kept_filtered),
                (long_out, kept_long_out),
                (own_spectra, kept_spectra),
            ],
            semaphores,
        )
    )


def backward_kernel(
    kept_spectra, kept_filtered, kept_long_out, kept_own_spectra,
    kept_one, kept_slope_one, kept_two, kept_slope_two,
    blocks, params, features, filter_mid, table_high, table_low, back_high, back_low,
    kept_grad_streams, grad_shared, grad_last,
    spectra, filtered, long_out, own_spectra, hidden_one, slope_one, hidden_two, slope_two,
    grad_streams, sums, lag_sums, grad_spectra, semaphores,
):
    copies = start_copies(
        [
            (kept_filtered, filtered),
            (kept_spectra, spectra),
            (kept_own_spectra, own_spectra),
            (kept_long_out, long_out),
            (kept_two, hidden_two),
            (kept_slope_two, slope_two),
            (kept_one, hidden_one),
            (kept_slope_one, slope_one),
        ],
        semaphores,
    )
    count = blocks.shape[0]
    hidden = filter_mid.shape[0]
    wide = 3 * ROWS
    grad_gated = blocks[...].astype(f32)[:, ROWS : 2 * ROWS, :]
    wait_copies(copies[:4])
    query = filtered[:, :ROWS, :]
    grad_long = (grad_gated * query).reshape(count * ROWS, BLOCK).astype(bf16)
    spectrum = table_dot(grad_long, table_high[...], table_low[...])
    grad_spectra[...] = rows_of(spectrum, ROWS)
    sign = parity()
    after = None
    for block in reversed(range(count)):
        back_real = jnp.zeros((ROWS, BLOCK), f32)
        back_imag = jnp.zeros((ROWS, BLOCK), f32)
        lag_real = jnp.zeros((ROWS, BLOCK), f32)
        lag_imag = jnp.zeros((ROWS, BLOCK), f32)
        for target in range(block, count):
            grad_real = grad_spectra[target, :, :BLOCK]
            grad_imag = grad_spectra[target, :, BLOCK:]
            filter_real = spectra[target - block, :, :BLOCK]
            filter_imag = spectra[target - block, :, BLOCK:]
            back_real = back_real + filter_real * grad_real + filter_imag * grad_imag
            back_imag = back_imag + filter_real * grad_imag - filter_imag * grad_real
            own_real = own_spectra[target - block, :, :BLOCK]
            own_imag = own_spectra[target - block, :, BLOCK:]
            lag_real = lag_real + own_real * grad_real + own_imag * grad_imag
            lag_imag = lag_imag + own_real * grad_imag - own_imag * grad_real
        at = slice(block * ROWS, (block + 1) * ROWS)
        sums[at, :BLOCK] = back_real
        sums[at, BLOCK:] = back_imag
        if after is None:
            lag_sums[at, :BLOCK] = lag_real
            lag_sums[at, BLOCK:] = lag_imag
        else:
            lag_sums[at, :BLOCK] = lag_real + sign * after[1]
            lag_sums[at, BLOCK:] = lag_imag - sign * after[0]
        after = (lag_real, lag_imag)
    back = table_dot(sums[...], back_high[...], back_low[...])
    skip = params[:, SKIP : SKIP + 1][None]
    grad_product = rows_of(back, ROWS) + skip * rows_of(grad_long.astype(f32), ROWS)
    grads = [
        grad_gated * long_out[...],
        grad_product * filtered[:, 2 * ROWS :, :],
        grad_product * filtered[:, ROWS : 2 * ROWS, :],
    ]
    lane = lax.broadcasted_iota(jnp.int32, (count * ROWS, BLOCK), 1)
    tail = jnp.zeros((ROWS, BLOCK), f32)
    adjoint = []
    for stream in range(3):
        value = grads[stream].reshape(count * ROWS, BLOCK)
        total = params[:, stream * 3 : stream * 3 + 1][None] * grads[stream]
        for by in (1, 2):
            rolled = pltpu.roll(value, BLOCK - by, 1)
            following = jnp.concatenate([rolled[ROWS:], tail], axis=0)
            moved = jnp.where(lane >= BLOCK - by, following, rolled)
            column = stream * 3 + by
            total = total + params[:, column : column + 1][None] * rows_of(moved, ROWS)
        adjoint.append(total)
    half = BLOCK // 2
    packed = [part[:, :, :half] for part in adjoint] + [part[:, :, half:] for part in adjoint]
    grad_streams[...] = jnp.concatenate(packed, axis=1).astype(bf16)
    streams_copy = pltpu.make_async_copy(grad_streams, kept_grad_streams, semaphores.at[8])
    streams_copy.start()
    wait_copies(copies[4:])

    lags = table_dot(lag_sums[...], back_high[...], back_low[...])
    decay = params[:, DECAY : DECAY + 1]
    last = params[:, OUT : OUT + hidden]
    raw = [
        lags[block * ROWS : (block + 1) * ROWS] * envelope(decay, block)
        for block in range(count)
    ]
    total_last = jnp.zeros((ROWS, hidden), f32)
    total_mid = jnp.zeros((hidden, hidden), f32)
    total_in = jnp.zeros((features.shape[0], hidden), f32)
    across = ((1,), (1,))
    for block in range(count):
        at = slice(block * BLOCK, (block + 1) * BLOCK)
        total_last = total_last + close_dot(raw[block], hidden_two[:, at], across)
        grad_two = close_dot(last, raw[block], ((0,), (0,))) * slope_two[:, at]
        total_mid = total_mid + close_dot(hidden_one[:, at], grad_two, across)
        grad_one = close_dot(filter_mid[...], grad_two) * slope_one[:, at]
        total_in = total_in + close_dot(features[:, at], grad_one, across)
    grad_shared[...] = jnp.concatenate([total_in, total_mid], axis=0)
    high, low = halves(total_last)
    grad_last[...] = jnp.concatenate([high.astype(f32), low.astype(f32)], axis=0).astype(bf16)
    streams_copy.wait()


def pack_kernel(far_weight, far_cotangent, packed, weight, cotangent, semaphores):
    wait_copies(
        start_copies([(far_weight, weight), (far_cotangent, cotangent)], semaphores)
    )
    side = packed.shape[0]
    channels, tokens = cotangent.shape
    for i in range(side):
        packed[i, :, :tokens] = cotangent[...]
        pieces = [
            weight[:, (a * side + i) * channels : (a * side + i + 1) * channels]
            for a in range(side)
        ]
        packed[i, :, tokens:] = jnp.concatenate(pieces, axis=1)


NEAR, FAR = pltpu.VMEM, pltpu.HBM


def call(kernel, outs, scratch, copies, *operands):
    semaphores = [pltpu.SemaphoreType.DMA((copies,))] if copies else []
    return pl.pallas_call(
        kernel,
        out_shape=[
            pltpu.HBM(shape, kind) if place is FAR else jax.ShapeDtypeStruct(shape, kind)
            for place, shape, kind in outs
        ],
        in_specs=[pl.BlockSpec(memory_space=place) for place, _ in operands],
        out_specs=[pl.BlockSpec(memory_space=place) for place, _, _ in outs],
        scratch_shapes=[pltpu.VMEM(shape, kind) for shape, kind in scratch] + semaphores,
        compiler_params=pltpu.CompilerParams(vmem_limit_bytes=VMEM_LIMIT),
    )(
        *[
            pltpu.with_memory_space_constraint(operand, FAR) if place is FAR else operand
            for place, operand in operands
        ]
    )


def exchange(value, axis, groups=None):
    return lax.all_to_all(value, axis, 0, 0, tiled=True, axis_index_groups=groups)


def shards(
    streams, short_taps, filter_in, filter_mid, filter_out, decay_rate, skip_gain, out_weight,
    grad_out,
):
    channels, tokens = streams.shape[1:]
    blocks = lax.axis_size("ctx")
    owners = lax.axis_size("ch")
    me = lax.axis_index("ctx")
    length = blocks * tokens
    share = channels // blocks
    hidden = filter_in.shape[1]
    band_rows = filter_in.shape[0]
    side = int(math.isqrt(owners))
    near_groups = [[a * side + i for i in range(side)] for a in range(side)]
    far_groups = [[a * side + i for a in range(side)] for i in range(side)]
    places = side // 2
    place_groups = [group[h * places : (h + 1) * places] for group in far_groups for h in range(2)]
    half = lax.axis_index("ch") // (places * side)

    def other_half(value):
        pairs = [(j, (j + places * side) % owners) for j in range(owners)]
        return lax.ppermute(value, "ch", pairs)

    chips = blocks // 2
    core = me % 2
    core_pairs = [(k, k ^ 1) for k in range(blocks)]
    chip_groups = [[2 * z + c for z in range(chips)] for c in range(2)]

    def in_order(here, there):
        second = core == 1
        return [jnp.where(second, there, here), jnp.where(second, here, there)]

    def between_cores(value, axis):
        here = lax.dynamic_index_in_dim(value, core, axis, False)
        there = lax.dynamic_index_in_dim(value, 1 - core, axis, False)
        return in_order(here, lax.ppermute(there, "ctx", core_pairs))
    group = side * channels
    pad_rows = ROWS - share
    tables = [jnp.asarray(t) for t in transform_tables()]
    features = jnp.asarray(position_features(band_rows // 2, length))

    (sent,) = call(
        pack_kernel,
        [(NEAR, (side, channels, tokens + group), bf16)],
        [(out_weight.shape, bf16), (grad_out.shape, bf16)],
        2,
        (FAR, out_weight), (FAR, grad_out),
    )
    sent = exchange(sent, "ch", near_groups)
    cotangent = sent[:, :, :tokens].reshape(group, tokens)
    weight = sent[:, :, tokens:].reshape(group, group)
    grad_terms = lax.dot_general(
        weight, cotangent, (((0,), (0,)), ((), ())), preferred_element_type=f32
    ).astype(bf16)
    grad_terms = between_cores(grad_terms.reshape(side, chips, 2, share, tokens), 2)
    grad_terms = jnp.stack(grad_terms, axis=1).reshape(2, places, channels, tokens)
    grad_terms = exchange(grad_terms.transpose(1, 0, 2, 3), "ch", place_groups)
    grad_terms = jnp.sum(grad_terms.astype(f32), axis=0)
    received = other_half(lax.dynamic_index_in_dim(grad_terms, 1 - half, 0, False).astype(bf16))
    grad_gated = lax.dynamic_index_in_dim(grad_terms, half, 0, False)
    grad_gated = (grad_gated + received.astype(f32)).astype(bf16)

    params = jnp.concatenate(
        [
            short_taps.transpose(1, 0, 2).reshape(channels, 9),
            decay_rate[:, None],
            skip_gain[:, None],
            filter_out.T,
        ],
        axis=1,
    )
    params = lax.dynamic_slice_in_dim(params, me * share, share, 0)
    params = jnp.pad(params, ((0, pad_rows), (0, 128 - params.shape[1])))

    def near(*values):
        return [(NEAR, value) for value in values]

    def far_like(shapes):
        return [(FAR,) + shape for shape in shapes]

    wave = ((hidden, length), f32)
    spectrum = ((blocks, ROWS, 2 * tokens), f32)
    kept_waves = [wave] * 4 + [spectrum]
    *waves, spectra = call(
        network_kernel, far_like(kept_waves), kept_waves + [((blocks * ROWS, tokens), f32)], 5,
        *near(features, filter_in, filter_mid, params, tables[0], tables[1]),
    )

    by_share = streams.reshape(3, blocks, share, tokens).transpose(1, 0, 2, 3)
    by_share = jnp.pad(by_share, ((0, 0), (0, 0), (0, pad_rows), (0, 0)))
    by_share = between_cores(by_share.reshape(chips, 2, 3 * ROWS, tokens), 1)
    by_share = jnp.concatenate(by_share, axis=1)
    by_share, spectra = lax.optimization_barrier((by_share, spectra))
    sequence = exchange(by_share, "ctx", chip_groups).reshape(blocks, 3 * ROWS, tokens)
    kept = [
        ((blocks * ROWS, tokens), bf16),
        ((blocks, 3 * ROWS, tokens), f32),
        ((blocks, ROWS, tokens), f32),
        spectrum,
    ]
    gated, filtered, long_out, own_spectra = call(
        forward_kernel, far_like(kept), kept + [((blocks * ROWS, 2 * tokens), f32)], 4,
        *near(sequence, params, spectra, *tables),
    )

    turned = grad_gated.reshape(2, chips, share, tokens).transpose(1, 0, 2, 3)
    turned = jnp.pad(turned, ((0, 0), (0, 0), (0, pad_rows), (0, 0)))
    first, second = between_cores(gated.reshape(chips, 2, ROWS, tokens), 1)
    turned = jnp.concatenate([first, turned[:, 0], second, turned[:, 1]], axis=1)
    turned = exchange(turned, "ctx", chip_groups).reshape(blocks, 2 * ROWS, tokens)
    own_gated = turned[:, :share, :].reshape(channels, tokens)
    all_gated = exchange(
        jnp.broadcast_to(own_gated[None], (side, channels, tokens)), "ch", far_groups
    ).reshape(group, tokens)

    packed_streams = ((blocks, 6 * ROWS, tokens // 2), bf16)
    grad_packed, grad_shared, grad_last = call(
        backward_kernel,
        [
            (FAR,) + packed_streams,
            (NEAR, (band_rows + hidden, hidden), f32),
            (NEAR, (2 * ROWS, hidden), bf16),
        ],
        [spectrum, kept[1], kept[2], spectrum]
        + [wave] * 4
        + [packed_streams]
        + [((blocks * ROWS, 2 * tokens), f32)] * 2
        + [spectrum],
        9,
        *[(FAR, value) for value in (spectra, filtered, long_out, own_spectra, *waves)],
        *near(turned, params, features, filter_mid, *tables),
    )

    shared = grad_shared
    for stride in (side, 2 * side, 4 * side):
        pairs = [(j, j ^ stride) for j in range(owners)]
        shared = shared + lax.ppermute(shared, "ch", pairs)

    out_terms = jnp.dot(weight, all_gated, preferred_element_type=f32).astype(bf16)
    def both_halves(value):
        high = lax.reduce_precision(value, 8, 7)
        return high.astype(bf16), (value - high).astype(bf16)

    rows = side * share
    portion = (band_rows + hidden) // blocks
    by_core = cotangent.reshape(side, chips, 2, share, tokens).transpose(2, 1, 0, 3, 4)
    shared = shared.reshape(chips, 2, portion, hidden)
    grad_packed = grad_packed.reshape((chips, 2) + grad_packed.shape[1:])

    def parts_for(which):
        left = lax.dynamic_index_in_dim(by_core, which, 0, False).reshape(chips * rows, tokens)
        terms = lax.dot_general(
            left, all_gated, (((1,), (1,)), ((), ())), preferred_element_type=f32
        ).reshape(chips, rows, group)
        return (
            terms,
            lax.dynamic_index_in_dim(shared, which, 1, False),
            lax.dynamic_index_in_dim(grad_packed, which, 1, False),
        )

    def joined(terms, shared, lasts, packed):
        high, low = both_halves(shared)
        small = jnp.concatenate([high, low] + lasts, axis=1)
        small = jnp.pad(small, ((0, 0), (0, rows - small.shape[1]), (0, 0)))
        return jnp.concatenate([terms.astype(bf16), small] + packed, axis=2)

    last_here = jnp.broadcast_to(grad_last[None], (chips,) + grad_last.shape)
    terms, shared_part, packed = parts_for(1 - core)
    sent = joined(terms, shared_part, [last_here], [packed])
    sent = lax.ppermute(sent, "ctx", core_pairs)
    terms, shared_part, packed = parts_for(core)
    terms = terms + sent[:, :, :group].astype(f32)
    small = sent[:, :, group : group + hidden]
    shared_part = (
        shared_part
        + small[:, :portion].astype(f32)
        + small[:, portion : 2 * portion].astype(f32)
    )
    last_at = 2 * portion
    last_there = small[:, last_at : last_at + 2 * ROWS]
    packed_there = sent[:, :, group + hidden :]
    sent = joined(
        terms, shared_part, in_order(last_here, last_there), in_order(packed, packed_there)
    )
    sent = exchange(sent, "ctx", chip_groups)
    weight_share = jnp.sum(sent[:, :, :group].astype(f32), axis=0).astype(bf16)
    small = sent[:, :, group : group + hidden].astype(f32)
    shared = jnp.sum(small[:, :portion] + small[:, portion : 2 * portion], axis=0)
    lasts = small[:, last_at : last_at + 4 * ROWS].reshape(blocks, 2, ROWS, hidden)[:, :, :share]
    grad_filter_out = jnp.sum(lasts, axis=1).reshape(channels, hidden).T
    packed = sent[:, :, group + hidden :].reshape(chips, 2, 3, ROWS, 2, tokens // 2)
    grad_streams = (
        packed[:, :, :, :share].transpose(2, 0, 4, 3, 1, 5).reshape(3, channels, tokens)
    )

    high, low = both_halves(shared)
    width = 3 * tokens
    tail = jnp.concatenate([high, low], axis=0).reshape(2 * portion * hidden // tokens, tokens)
    weight_rows = jnp.pad(
        weight_share.reshape(side, share, group), ((0, 0), (0, 0), (0, width - group))
    ).reshape(side, share * 3, tokens)
    sent = jnp.concatenate(
        [
            out_terms.reshape(side, channels, tokens),
            weight_rows,
            jnp.broadcast_to(tail[None], (side,) + tail.shape),
        ],
        axis=1,
    )
    sent = exchange(sent, "ch", near_groups)
    layer_out = jnp.sum(sent[:, :channels].astype(f32), axis=0).astype(bf16)
    weight_rows = sent[:, channels : channels + 3 * share].reshape(side, share, width)[:, :, :group]
    weight_rows = weight_rows.reshape(side, share, side, channels).transpose(1, 2, 0, 3)
    weight_rows = weight_rows.reshape(share, owners * channels)
    tail = jnp.sum(sent[:, channels + 3 * share :].astype(f32), axis=0)
    tail = tail.reshape(2, portion * hidden)
    high, low = both_halves(tail[0] + tail[1])

    tail = jnp.concatenate([high, low])
    spare = -tail.size % (share * 128)
    tail = jnp.pad(tail, (0, spare)).reshape(share, -1)
    sent = lax.all_gather(jnp.concatenate([weight_rows, tail], axis=1), "ctx", axis=0)
    grad_out_weight = sent[:, :, : weight_rows.shape[1]].reshape(channels, -1).astype(f32)
    tail = sent[:, :, weight_rows.shape[1] :].reshape(blocks, -1).astype(f32)
    size = portion * hidden
    shared = (tail[:, :size] + tail[:, size : 2 * size]).reshape(band_rows + hidden, hidden)
    return (
        layer_out, grad_streams, shared[:band_rows], shared[band_rows:], grad_filter_out,
        grad_out_weight,
    )


def solution(mesh):
    return jax.shard_map(
        shards,
        mesh=mesh,
        in_specs=(
            P(None, "ch", "ctx"),
            P(None, "ch", None),
            P(),
            P(),
            P(None, "ch"),
            P("ch"),
            P("ch"),
            P("ch", None),
            P("ch", "ctx"),
        ),
        out_specs=(P("ch", "ctx"), P(None, "ch", "ctx"), P(), P(), P(None, "ch"), P("ch", None)),
        check_vma=False,
    )
```
